128 devices in a mesh: grp: 8 (over z, core), blk: 16 (over y, x).
Axes of the slice: x: 4, y: 4, z: 4, core: 2. Of those that a mesh axis runs over, the one named last changes fastest.
Arguments:
- matrix: float32 [32768, 4096], P(('grp', 'blk')), as said below
- signs: int32 [32768], P(('grp', 'blk')), may hold values from -1 to 1, as said below
- tile_rows: int32 [8, 16, 128], P('grp'), may hold values from -1 to 255, as said below
- tile_owner: int32 [8, 16], P('grp'), may hold values from 0 to 15, as said below
Outputs:
- r_top: float32 [768, 4096], P(None, 'blk')
- trailing: float32 [32768, 4096], P(('grp', 'blk'))
The draws below stay inside these ranges and needn't reach their ends.
Inputs may be any that keep to these rules, and one draw needn't show every extreme that they name: `tile_rows`: slot s of every tile samples a row of the device at blk index s mod 16 of the same grp index; each grp index has padding and reaches the largest row index. `tile_owner`: within each grp index no owner holds more than 2 tiles, and some owner holds exactly 2. `signs`: each entry is -1 or 1. `matrix`: entries of order one with per-column scales.
All inputs are finite; a program needn't handle non-finite values.
Results may differ from the reference program's by a relative error of at most 0.0001.
Values sent between devices are 32-bit elements; how exact they have to be, the bound alone decides.
No kernel may reach another device: no remote copies, remote signals or barrier semaphores. Data moves between devices by JAX's collectives and lax.ppermute only.
A program may use at most 128 MiB of HBM per device.

```python
import math
import jax
import jax.numpy as jnp
from jax import lax

D = 4096
ROWS_DEV = 256
TILE = 128
MAXT = 2
PANEL = 128
NPAN = 6
ROWS = 32768
SLOTS = 32768
N_GRP = 8
N_BLK = 16


def draw_matrix(key, part):
    key = jax.random.fold_in(key, 11)
    first, second = jax.random.split(key, 2)
    col_scale = jnp.exp(jax.random.uniform(second, (D,), jnp.float32, math.log(0.3), math.log(3.0)))
    values = jax.random.normal(first, (ROWS, D), jnp.float32) * col_scale[None, :]
    return values.astype(jnp.float32)


def draw_signs(key, part):
    key = jax.random.fold_in(key, 12)
    return (2 * jax.random.randint(key, (ROWS,), 0, 2) - 1).astype(jnp.int32)


def draw_tile_rows(key, part):
    key = jax.random.fold_in(key, 13)
    first, second = jax.random.split(key)
    rows = jax.random.randint(first, (N_GRP, N_BLK, TILE), 0, ROWS_DEV)
    padded = jax.random.randint(second, (N_GRP, N_BLK, TILE), 0, 5) == 0
    rows = jnp.where(padded, -1, rows)
    rows = rows.at[:, 0, 0].set(ROWS_DEV - 1)
    rows = rows.at[:, 0, 1].set(-1)
    return rows.astype(jnp.int32)


def owners_of_group(key):
    first, second, third = jax.random.split(key, 3)
    rest = jax.random.permutation(first, jnp.arange(MAXT, MAXT * N_BLK, dtype=jnp.int32))[:N_BLK - MAXT]
    places = jnp.concatenate([jnp.arange(MAXT, dtype=jnp.int32), rest])
    places = jax.random.permutation(second, places)
    relabel = jax.random.permutation(third, jnp.arange(N_BLK, dtype=jnp.int32))
    return relabel[places // MAXT]


def draw_tile_owner(key, part):
    key = jax.random.fold_in(key, 14)
    keys = jax.random.split(key, N_GRP)
    return jax.vmap(owners_of_group)(keys).astype(jnp.int32)


def setup_inputs(seed: int = 0) -> dict:
    seeds = jax.random.split(jax.random.key(seed), 5)
    matrix = draw_matrix(jax.random.fold_in(seeds[4], 71), 0)
    signs = draw_signs(jax.random.fold_in(seeds[4], 71), 0)
    tile_rows = draw_tile_rows(jax.random.fold_in(seeds[4], 71), 0)
    tile_owner = draw_tile_owner(jax.random.fold_in(seeds[4], 71), 0)
    return {"matrix": matrix, "signs": signs, "tile_rows": tile_rows, "tile_owner": tile_owner}


def hadamard(order):
    index = jnp.arange(order, dtype=jnp.int32)
    total = jnp.zeros((order, order), jnp.int32)
    for level in range(order.bit_length() - 1):
        upper = index // 2 ** level % 2
        total = total + upper[:, None] * upper[None, :]
    return (1 - 2 * (total % 2)).astype(jnp.float32)

def lower_solve(lower, right):
    return lax.linalg.triangular_solve(lower, right, left_side=True, lower=True)

def reference(matrix, signs, tile_rows, tile_owner):
    signed = matrix * signs.astype(jnp.float32)[:, None]
    blocks = signed.reshape(N_GRP, N_BLK, ROWS_DEV, D)
    local = jnp.einsum('ij,gbjd->gbid', hadamard(ROWS_DEV), blocks, precision=lax.Precision.HIGHEST)
    mixed = jnp.einsum('hg,gbid->hbid', hadamard(N_GRP), local, precision=lax.Precision.HIGHEST)
    mixed = mixed * (1.0 / math.sqrt(N_GRP * ROWS_DEV))
    source = jnp.arange(TILE, dtype=jnp.int32) % N_BLK
    safe_rows = jnp.maximum(tile_rows, 0)
    group_index = jnp.arange(N_GRP, dtype=jnp.int32)[:, None, None]
    values = mixed[group_index, source[None, None, :], safe_rows]
    values = jnp.where((tile_rows >= 0)[..., None], values, 0.0)
    same = tile_owner[:, :, None] == tile_owner[:, None, :]
    tiles = jnp.arange(N_BLK, dtype=jnp.int32)
    earlier = tiles[None, :] < tiles[:, None]
    rank = lax.optimization_barrier(jnp.sum((same & earlier[None]).astype(jnp.int32), axis=2))
    target = ((jnp.arange(N_GRP, dtype=jnp.int32)[:, None] * N_BLK + tile_owner) * MAXT + rank).astype(jnp.int32)
    sketch = jnp.zeros((N_GRP * N_BLK * MAXT, TILE, D), jnp.float32)
    sketch = sketch.at[target.reshape(-1)].set(values.reshape(N_GRP * N_BLK, TILE, D))
    current = sketch.reshape(SLOTS, D)
    columns = jnp.arange(D, dtype=jnp.int32)
    factor_rows = []
    for panel_index in range(NPAN):
        start = panel_index * PANEL
        panel = current[:, start:start + PANEL]
        products = jnp.dot(panel.T.astype(jnp.float32), current.astype(jnp.float32), precision=lax.Precision.HIGHEST, preferred_element_type=jnp.float32)
        lower = jnp.linalg.cholesky(products[:, start:start + PANEL])
        row_block = lower_solve(lower, products)
        row_block = jnp.where(columns[None, :] >= start, row_block, 0.0)
        basis = lower_solve(lower, panel.T).T
        current = current - jnp.dot(basis.astype(jnp.float32), row_block.astype(jnp.float32), precision=lax.Precision.HIGHEST, preferred_element_type=jnp.float32)
        factor_rows.append(row_block)
    r_top = jnp.concatenate(factor_rows, axis=0) * (1.0 / math.sqrt(N_GRP * N_BLK * TILE))
    return (r_top, current)
```

```python
import functools
import math

import jax
import jax.numpy as jnp
from jax import lax
from jax.experimental import pallas as pl
from jax.experimental.pallas import tpu as pltpu
from jax.sharding import PartitionSpec as P

TILE = 128
MAXT = 2
PANEL = 128
NPAN = 6
WIDE = PANEL * NPAN
HI = lax.Precision.HIGHEST


def dot(a, b, dims, precision=HI):
    return lax.dot_general(
        a, b, (dims, ((), ())), precision=precision, preferred_element_type=jnp.float32
    )


def inverse_factor(block):
    n = block.shape[0]
    sub = lax.broadcasted_iota(jnp.int32, (n, n), 0)
    lane = lax.broadcasted_iota(jnp.int32, (n, n), 1)
    sub8 = lax.broadcasted_iota(jnp.int32, (8, n), 0)
    left, right = block, (sub == lane).astype(jnp.float32)
    rows = []
    for step in range(n // 8):
        base = 8 * step
        top_left, top_right = left[:8], right[:8]
        cols = [jnp.broadcast_to(top_left[:, base + k : base + k + 1], (8, n)) for k in range(8)]
        pivots = jnp.zeros((8, n), jnp.float32)
        for j in range(8):
            pivot = jnp.broadcast_to(cols[j][j : j + 1], (8, n))
            pivots = jnp.where(sub8 == j, pivot, pivots)
            if j == 7:
                break
            factor = jnp.where(sub8 > j, cols[j] * (1.0 / pivot), 0.0)
            for k in range(j + 1, 8):
                cols[k] = cols[k] - factor * cols[k][j : j + 1]
            top_left = top_left - factor * top_left[j : j + 1]
            top_right = top_right - factor * top_right[j : j + 1]
        scale = lax.rsqrt(pivots)
        top_left, top_right = top_left * scale, top_right * scale
        rows.append(top_right)
        if step < n // 8 - 1:
            turned = top_left.T
            left, right = left[8:], right[8:]
            for k in range(8):
                col = turned[base + 8 :, k : k + 1]
                left = left - col * top_left[k : k + 1]
                right = right - col * top_right[k : k + 1]
    return jnp.concatenate(rows, axis=0)


def factor_kernel(gram_ref, inv_ref, work_ref):
    n = gram_ref.shape[0]
    work_ref[...] = gram_ref[...]
    inv_ref[...] = jnp.zeros_like(inv_ref)
    for low in range(0, n, PANEL):
        high = low + PANEL
        inverse = inverse_factor(work_ref[low:high, low:high])
        inv_ref[low:high, low:high] = inverse
        if low:
            inv_ref[low:high, :low] = dot(inverse, inv_ref[low:high, :low], ((1,), (0,)))
        if high < n:
            upper = dot(inverse, work_ref[low:high, high:], ((1,), (0,)))
            work_ref[high:, high:] -= dot(upper, upper, ((0,), (0,)))
            inv_ref[high:, :high] -= dot(upper, inv_ref[low:high, :high], ((0,), (0,)))


def inverse_of_factor(gram):
    n = gram.shape[0]
    return pl.pallas_call(
        factor_kernel,
        out_shape=jax.ShapeDtypeStruct((n, n), jnp.float32),
        in_specs=[pl.BlockSpec(memory_space=pltpu.VMEM)],
        out_specs=pl.BlockSpec(memory_space=pltpu.VMEM),
        scratch_shapes=[pltpu.VMEM((n, n), jnp.float32)],
        compiler_params=pltpu.CompilerParams(vmem_limit_bytes=32 * 2**20),
        cost_estimate=pl.CostEstimate(flops=10**9, bytes_accessed=6 * 2**20, transcendentals=0),
    )(gram)


def grp_swap(x, d):
    return lax.ppermute(x, "grp", [(i, i ^ d) for i in range(lax.axis_size("grp"))])


def parity(x):
    return lax.population_count(x) % 2


def body(matrix, signs, tile_rows, tile_owner):
    rows_dev, width = matrix.shape
    groups = lax.axis_size("grp")
    owners = lax.axis_size("blk")
    me = lax.axis_index("grp")
    me_blk = lax.axis_index("blk")
    zed, core = me // 2, me % 2
    tiles = tile_owner.shape[1]
    per_source = TILE // owners
    lanes = 128
    slots = width // (groups * lanes)
    part = slots * lanes
    picked = tiles * per_source

    wanted = tile_rows[0].reshape(tiles, per_source, owners)
    selector = jnp.arange(owners, dtype=jnp.int32) == me_blk
    wanted = jnp.sum(jnp.where(selector, wanted, 0), axis=2).reshape(1, picked)
    wanted = lax.all_gather(wanted, "grp", tiled=True)

    signed = matrix * signs.astype(jnp.float32)[:, None]
    pieces = signed.reshape(rows_dev, slots, groups // 2, 2, lanes).transpose(2, 3, 0, 1, 4)
    pieces = pieces.reshape(groups // 2, 2, rows_dev, part)
    got = []
    for d in range(groups // 2):
        mine = lax.dynamic_index_in_dim(pieces, zed ^ d, 0, keepdims=False)
        got.append(grp_swap(mine, 2 * d) if d else mine)
    got = jnp.stack(got)
    keep = lax.dynamic_index_in_dim(got, core, 1, keepdims=False)
    give = lax.dynamic_index_in_dim(got, 1 - core, 1, keepdims=False)
    mixed = jnp.stack([keep, grp_swap(give, 1)], axis=1).reshape(groups, rows_dev, part)
    for level in range(groups.bit_length() - 1):
        mixed = mixed.reshape(groups >> (level + 1), 2, 1 << level, rows_dev, part)
        low, high = mixed[:, 0], mixed[:, 1]
        mixed = jnp.stack([low + high, low - high], axis=1)
    mixed = mixed.reshape(groups, rows_dev, part)

    index = jnp.arange(rows_dev, dtype=jnp.int32)
    odd = parity(jnp.maximum(wanted, 0)[:, :, None] & index)
    odd = odd + parity(jnp.arange(groups, dtype=jnp.int32) & me)[:, None, None]
    select = (1 - 2 * (odd % 2)).astype(jnp.float32)
    select = jnp.where((wanted >= 0)[:, :, None], select, 0.0)
    sampled = jnp.einsum(
        "gsi,gic->gsc", select, mixed, precision=HI, preferred_element_type=jnp.float32
    ) * (1.0 / math.sqrt(groups * rows_dev))

    mine = sampled[:, :, :lanes]
    got = jnp.stack([grp_swap(mine, 2 * d) if d else mine for d in range(groups // 2)])
    got = jnp.stack([got, grp_swap(got, 1)], axis=1).reshape(groups, groups * picked, lanes)
    lead = jnp.concatenate(
        [lax.dynamic_index_in_dim(got, me ^ t, 0, keepdims=False) for t in range(NPAN)], axis=1
    )

    rest = sampled.reshape(groups * picked, part)
    partial = dot(lead, rest, ((0,), (0,)))
    share = WIDE // owners
    partial = partial.reshape(owners, share, part)
    gram = jnp.sum(lax.all_to_all(partial, "blk", 0, 0, tiled=True), axis=0)
    corner = lax.all_gather(gram[:, :lanes], ("grp", "blk"), tiled=True)
    corner = corner.reshape(groups, WIDE, lanes)
    gram = lax.all_gather(gram, ("grp", "blk"), tiled=True).reshape(groups, WIDE, part)

    back = sampled.reshape(groups // 2, 2, picked, part)
    got = []
    for d in range(groups // 2):
        mine = lax.dynamic_index_in_dim(back, zed ^ d, 0, keepdims=False)
        got.append(grp_swap(mine, 2 * d) if d else mine)
    got = jnp.stack(got)
    keep = lax.dynamic_index_in_dim(got, core, 1, keepdims=False)
    give = lax.dynamic_index_in_dim(got, 1 - core, 1, keepdims=False)
    got = jnp.stack([keep, grp_swap(give, 1)], axis=1).reshape(groups, picked, slots, lanes)
    home = jnp.stack(
        [lax.dynamic_index_in_dim(got, me ^ t, 0, keepdims=False) for t in range(groups)], axis=2
    ).reshape(tiles, per_source, width)
    owner_list = tile_owner[0]
    same = owner_list[:, None] == owner_list[None, :]
    order = jnp.arange(tiles, dtype=jnp.int32)
    rank = jnp.sum((same & (order[None, :] < order[:, None])).astype(jnp.int32), axis=1)
    target = owner_list * MAXT + rank
    outgoing = jnp.zeros((owners * MAXT, per_source, width), jnp.float32).at[target].set(home)
    outgoing = outgoing.reshape(owners, MAXT, per_source, 1, width)
    arrived = lax.all_to_all(outgoing, "blk", split_axis=0, concat_axis=3, tiled=True)
    current = arrived.reshape(MAXT * TILE, width)

    corner = jnp.concatenate([corner[t] for t in range(NPAN)], axis=1)
    inverse = inverse_of_factor(corner)
    basis = dot(current[:, :WIDE], inverse, ((1,), (1,)))
    weights = dot(basis, inverse, ((1,), (0,)))
    taken = jnp.einsum(
        "rk,ckn->rcn", weights, gram, precision=HI, preferred_element_type=jnp.float32
    )
    taken = taken.reshape(MAXT * TILE, groups, slots, lanes).transpose(0, 2, 1, 3)
    trailing = current - taken.reshape(MAXT * TILE, width)

    wide = width // owners
    per = wide // lanes
    first = me_blk * per
    own = lax.dynamic_slice(
        gram, (first % groups, 0, first // groups * lanes), (per, WIDE, lanes)
    )
    own = own.transpose(1, 0, 2).reshape(WIDE, wide)
    r_top = dot(inverse, own, ((1,), (0,)))
    column = me_blk * wide + jnp.arange(wide, dtype=jnp.int32)
    start = jnp.arange(WIDE, dtype=jnp.int32) // PANEL * PANEL
    r_top = jnp.where(column[None, :] >= start[:, None], r_top, 0.0)
    r_top = r_top * (1.0 / math.sqrt(groups * owners * TILE))
    return (r_top, trailing)


def solution(mesh):
    in_specs = (P(("grp", "blk"), None), P(("grp", "blk")), P("grp", None, None), P("grp", None))
    out_specs = (P(None, "blk"), P(("grp", "blk"), None))
    return jax.shard_map(body, mesh=mesh, in_specs=in_specs, out_specs=out_specs, check_vma=False)
```

```python
import functools
import math

import jax
import jax.numpy as jnp
from jax import lax
from jax.experimental import pallas as pl
from jax.experimental.pallas import tpu as pltpu
from jax.sharding import PartitionSpec as P

TILE = 128
MAXT = 2
PANEL = 128
NPAN = 6
WIDE = PANEL * NPAN
LANES = 128
HI = lax.Precision.HIGHEST


def dot(a, b, dims, precision=HI):
    return lax.dot_general(
        a, b, (dims, ((), ())), precision=precision, preferred_element_type=jnp.float32
    )


def inverse_factor(block):
    n = block.shape[0]
    sub = lax.broadcasted_iota(jnp.int32, (n, n), 0)
    lane = lax.broadcasted_iota(jnp.int32, (n, n), 1)
    sub8 = lax.broadcasted_iota(jnp.int32, (8, n), 0)
    left, right = block, (sub == lane).astype(jnp.float32)
    rows = []
    for step in range(n // 8):
        base = 8 * step
        top_left, top_right = left[:8], right[:8]
        cols = [jnp.broadcast_to(top_left[:, base + k : base + k + 1], (8, n)) for k in range(8)]
        pivots = jnp.zeros((8, n), jnp.float32)
        for j in range(8):
            pivot = jnp.broadcast_to(cols[j][j : j + 1], (8, n))
            pivots = jnp.where(sub8 == j, pivot, pivots)
            if j == 7:
                break
            factor = jnp.where(sub8 > j, cols[j] * (1.0 / pivot), 0.0)
            for k in range(j + 1, 8):
                cols[k] = cols[k] - factor * cols[k][j : j + 1]
            top_left = top_left - factor * top_left[j : j + 1]
            top_right = top_right - factor * top_right[j : j + 1]
        scale = lax.rsqrt(pivots)
        top_left, top_right = top_left * scale, top_right * scale
        rows.append(top_right)
        if step < n // 8 - 1:
            turned = top_left.T
            left, right = left[8:], right[8:]
            for k in range(8):
                col = turned[base + 8 :, k : k + 1]
                left = left - col * top_left[k : k + 1]
                right = right - col * top_right[k : k + 1]
    return jnp.concatenate(rows, axis=0)


def factor_kernel(place_ref, own_ref, other_ref, inv_ref, corner_ref, work_ref):
    me, me_blk = place_ref[0], place_ref[1]
    quads, owners, share, lanes = own_ref.shape
    n = owners * share
    for tile in range(2 * quads):
        far = me ^ tile
        for owner in range(owners):
            rows = slice(owner * share, (owner + 1) * share)
            near = me_blk ^ owner
            piece = jnp.where(far % 2 == 0, own_ref[far // 2, near], other_ref[far // 2, near])
            corner_ref[tile, rows, :] = piece
            if tile * lanes < n:
                work_ref[rows, tile * lanes : (tile + 1) * lanes] = piece
    inv_ref[...] = jnp.zeros_like(inv_ref)
    for low in range(0, n, PANEL):
        high = low + PANEL
        inverse = inverse_factor(work_ref[low:high, low:high])
        inv_ref[low:high, low:high] = inverse
        if low:
            inv_ref[low:high, :low] = dot(inverse, inv_ref[low:high, :low], ((1,), (0,)))
        if high < n:
            upper = dot(inverse, work_ref[low:high, high:], ((1,), (0,)))
            work_ref[high:, high:] -= dot(upper, upper, ((0,), (0,)))
            inv_ref[high:, :high] -= dot(upper, inv_ref[low:high, :high], ((0,), (0,)))


def inverse_of_factor(place, own, other):
    quads, owners, share, lanes = own.shape
    n = owners * share
    return pl.pallas_call(
        factor_kernel,
        out_shape=(
            jax.ShapeDtypeStruct((n, n), jnp.float32),
            jax.ShapeDtypeStruct((2 * quads, n, lanes), jnp.float32),
        ),
        in_specs=[pl.BlockSpec(memory_space=pltpu.SMEM)]
        + [pl.BlockSpec(memory_space=pltpu.VMEM)] * 2,
        out_specs=(pl.BlockSpec(memory_space=pltpu.VMEM), pl.BlockSpec(memory_space=pltpu.VMEM)),
        scratch_shapes=[pltpu.VMEM((n, n), jnp.float32)],
        compiler_params=pltpu.CompilerParams(vmem_limit_bytes=32 * 2**20),
        cost_estimate=pl.CostEstimate(
            flops=40 * 10**9, bytes_accessed=100 * 2**20, transcendentals=0
        ),
    )(place, own, other)


def swap(x, axis, d):
    return lax.ppermute(x, axis, [(i, i ^ d) for i in range(lax.axis_size(axis))])


def exchange(pieces, core):
    kept = [swap(x, "grp", 2 * d) if d else x for d, x in enumerate(pieces)]
    other = [lax.dynamic_index_in_dim(x, 1 - core, 0, keepdims=False) for x in kept]
    return kept, [swap(x, "grp", 1) for x in other]


def parity(x):
    return lax.population_count(x) % 2


def split_kernel(quads, per, place_ref, sign_ref, *refs):
    sources, outs = refs[: quads * per], refs[quads * per :]
    sign = sign_ref[...].astype(jnp.float32)
    for d, out in enumerate(outs):
        half = out.shape[2]
        for s, source in enumerate(sources[d * per : (d + 1) * per]):
            signed = source[...] * sign
            for part in range(2):
                core, at = divmod((2 * s + part) * LANES, half)
                out[core, :, at : at + LANES] = signed[:, part * LANES : (part + 1) * LANES]


def split_columns(zed, matrix, signs, quads, first, part):
    rows = matrix.shape[0]
    block = 2 * LANES
    per = 2 * part // block
    reads = [
        pl.BlockSpec(
            (rows, block), lambda i, z, d=d, s=s: (0, first // block + (z[0] ^ d) * per + s)
        )
        for d in range(quads)
        for s in range(per)
    ]
    shape = (2, rows, part)
    return pl.pallas_call(
        functools.partial(split_kernel, quads, per),
        grid_spec=pltpu.PrefetchScalarGridSpec(
            num_scalar_prefetch=1,
            grid=(1,),
            in_specs=[pl.BlockSpec((rows, 1), lambda i, z: (0, 0))] + reads,
            out_specs=[pl.BlockSpec(shape, lambda i, z: (0, 0, 0))] * quads,
        ),
        out_shape=[jax.ShapeDtypeStruct(shape, jnp.float32)] * quads,
        compiler_params=pltpu.CompilerParams(vmem_limit_bytes=32 * 2**20),
        cost_estimate=pl.CostEstimate(
            flops=2 * quads * rows * part,
            bytes_accessed=16 * quads * rows * part,
            transcendentals=0,
        ),
    )(zed.reshape(1), signs.reshape(rows, 1), *[matrix] * (quads * per))


def sample_kernel(scale, quads, has_early, place_ref, select_ref, *refs):
    mixed_ref = refs[-1]
    groups, rows, width = mixed_ref.shape
    kept, given = refs[:quads], refs[quads : 2 * quads]
    early_ref = refs[2 * quads] if has_early else None
    sampled_ref = refs[2 * quads + has_early]
    backs = refs[2 * quads + has_early + 1 : -1]
    step = 16 if width <= 128 else 8

    def mix(r, carry):
        at = pl.ds(pl.multiple_of(r * step, step), step)
        parts = []
        for d in range(quads):
            parts += [kept[d][0, at, :], given[d][at, :]]
        level = 1
        while level < groups:
            new = list(parts)
            for k in range(groups):
                if not k & level:
                    new[k] = parts[k] + parts[k | level]
                    new[k | level] = parts[k] - parts[k | level]
            parts = new
            level *= 2
        for k in range(groups):
            mixed_ref[k, at, :] = parts[k]
        return carry

    lax.fori_loop(0, rows // step, mix, 0)
    zed = place_ref[0] // 2
    for d in range(quads):
        for c in range(2):
            group = 2 * (zed ^ d) + c
            left = select_ref[group]
            value = mixed_ref[group]
            total = None
            for _ in range(3):
                high = value.astype(jnp.bfloat16)
                term = jnp.dot(left, high, preferred_element_type=jnp.float32)
                total = term if total is None else total + term
                value = value - high.astype(jnp.float32)
            total = total * scale
            if early_ref is None:
                sampled_ref[group] = total
                continue
            early = early_ref[group]
            done = early.shape[1]
            sampled_ref[group, :, :done] = early
            sampled_ref[group, :, done:] = total
            backs[d][c, :, :done] = early
            backs[d][c, :, done:] = total


def sample(me, select, kept, given, early=None):
    groups, picked, rows = select.shape
    quads = groups // 2
    block = given[0].shape[1]

    def whole(*shape):
        return pl.BlockSpec(shape, lambda s, p: (0,) * len(shape))

    in_specs = [whole(groups, picked, rows)]
    in_specs += [pl.BlockSpec((1, rows, block), lambda s, p: (p[0] % 2, 0, 0))] * quads
    in_specs += [whole(rows, block)] * quads
    shapes = [(groups, picked, block)]
    if early is not None:
        in_specs.append(whole(*early.shape))
        part = block + early.shape[2]
        shapes = [(groups, picked, part)] + [(2, picked, part)] * quads
    return pl.pallas_call(
        functools.partial(
            sample_kernel, 1.0 / math.sqrt(groups * rows), quads, early is not None
        ),
        grid_spec=pltpu.PrefetchScalarGridSpec(
            num_scalar_prefetch=1,
            grid=(1,),
            in_specs=in_specs,
            out_specs=[whole(*shape) for shape in shapes],
            scratch_shapes=[pltpu.VMEM((groups, rows, block), jnp.float32)],
        ),
        out_shape=[jax.ShapeDtypeStruct(shape, jnp.float32) for shape in shapes],
        compiler_params=pltpu.CompilerParams(vmem_limit_bytes=40 * 2**20),
        cost_estimate=pl.CostEstimate(
            flops=6 * groups * picked * rows * block, bytes_accessed=9 * 2**20, transcendentals=0
        ),
    )(me.reshape(1), select, *kept, *given, *([] if early is None else [early]))


def gram_kernel(place_ref, rest_ref, *refs):
    leads, out_ref = refs[:-1], refs[-1]
    for k, lead in enumerate(leads):
        tile = place_ref[0] ^ k

        @pl.when(tile < NPAN)
        def _():
            at = pl.ds(pl.multiple_of(tile * LANES, LANES), LANES)
            out_ref[at, :] = dot(lead[...], rest_ref[...], ((0,), (0,)))


def gram_part(me, rest, leads):
    rows, part = rest.shape
    return pl.pallas_call(
        gram_kernel,
        out_shape=jax.ShapeDtypeStruct((WIDE, part), jnp.float32),
        in_specs=[pl.BlockSpec(memory_space=pltpu.SMEM)]
        + [pl.BlockSpec(memory_space=pltpu.VMEM)] * (1 + len(leads)),
        out_specs=pl.BlockSpec(memory_space=pltpu.VMEM),
        compiler_params=pltpu.CompilerParams(vmem_limit_bytes=32 * 2**20),
        cost_estimate=pl.CostEstimate(
            flops=12 * rows * WIDE * part, bytes_accessed=8 * 2**20, transcendentals=0
        ),
    )(me.reshape(1), rest, *leads)


def pack_kernel(place_ref, tile_ref, *refs):
    out_ref, given_ref = refs[-1], refs[-2]
    kept = refs[:-2]
    quads = len(kept)
    places, per, width = out_ref.shape
    groups = 2 * quads
    rest = width // groups - LANES
    me = place_ref[0]

    def fill(q, carry):
        tile = tile_ref[q]
        at = pl.ds(pl.multiple_of(jnp.maximum(tile, 0) * per, per), per)
        for d in range(quads):
            for e in range(2):
                rows = given_ref[d, at, :] if e else kept[d][0, at, :]
                rows = jnp.where(tile >= 0, rows, 0.0)
                far = me ^ (2 * d + e)
                where = pl.ds(pl.multiple_of(far * LANES, LANES), LANES)
                out_ref[q, :, where] = rows[:, :LANES]
                column = groups * LANES + far * rest
                where = pl.ds(pl.multiple_of(column, LANES), rest)
                out_ref[q, :, where] = rows[:, LANES:]
        return carry

    lax.fori_loop(0, places, fill, 0)


def pack(me, tile_of, kept, given, per):
    places = tile_of.shape[0]
    quads, picked, part = given.shape
    width = 2 * quads * part
    whole = (quads, picked, part)
    return pl.pallas_call(
        pack_kernel,
        grid_spec=pltpu.PrefetchScalarGridSpec(
            num_scalar_prefetch=2,
            grid=(1,),
            in_specs=[pl.BlockSpec((1, picked, part), lambda s, p, t: (p[0] % 2, 0, 0))] * quads
            + [pl.BlockSpec(whole, lambda s, p, t: (0, 0, 0))],
            out_specs=pl.BlockSpec((places, per, width), lambda s, p, t: (0, 0, 0)),
        ),
        out_shape=jax.ShapeDtypeStruct((places, per, width), jnp.float32),
        compiler_params=pltpu.CompilerParams(vmem_limit_bytes=32 * 2**20),
        cost_estimate=pl.CostEstimate(flops=0, bytes_accessed=8 * 2**20, transcendentals=0),
    )(me.reshape(1), tile_of, *kept, given)


def halves(x):
    high = x.astype(jnp.bfloat16)
    return high, (x - high.astype(jnp.float32)).astype(jnp.bfloat16)


def product(weights, gram):
    high, low = halves(gram)

    def term(a, b):
        return jnp.dot(a, b, preferred_element_type=jnp.float32)

    return term(weights[0], high) + (term(weights[0], low) + term(weights[1], high))


def by_turn(value, owners):
    rows, columns = value.shape
    value = value.reshape(owners, rows // owners, columns)
    return jnp.swapaxes(value, 0, 1).reshape(rows, columns)


def lead_kernel(
    scale, owners, place_ref, current_ref, weights_ref, inverse_ref, gram_ref, trailing_ref, top_ref
):
    step = pl.program_id(0)
    gram = jnp.concatenate([gram_ref[0], gram_ref[1]], axis=1)
    taken = product(halves(weights_ref[...]), gram)
    trailing_ref[...] = by_turn(current_ref[...] - taken, owners)

    @pl.when(step == 0)
    def _():
        top_ref[...] = jnp.zeros_like(top_ref)

    @pl.when(step == place_ref[0])
    def _():
        top = dot(inverse_ref[...], gram, ((1,), (0,)))
        row = lax.broadcasted_iota(jnp.int32, top.shape, 0)
        column = lax.broadcasted_iota(jnp.int32, top.shape, 1) + step * top.shape[1]
        top_ref[...] = jnp.where(column >= row // PANEL * PANEL, top, 0.0) * scale


def rest_kernel(
    scale, owners, before, place_ref, current_ref, weights_ref, inverse_ref, gram_ref, lead_ref,
    trailing_in, trailing_ref, top_ref, split_ref, out_ref, sems
):
    step, steps = pl.program_id(0), pl.num_programs(0)
    part = gram_ref.shape[2]
    slot = lax.rem(step, 2)

    def send(step, slot):
        columns = pl.ds(pl.multiple_of(before + step * part, LANES), part)
        return pltpu.make_async_copy(out_ref.at[slot], trailing_ref.at[:, columns], sems.at[slot])

    @pl.when(step == 0)
    def _():
        split_ref[0], split_ref[1] = halves(weights_ref[...])
        top_ref[...] = lead_ref[...]

    @pl.when(step >= 2)
    def _():
        send(step - 2, slot).wait()

    columns = pl.ds(pl.multiple_of(before + step * part, LANES), part)
    taken = product((split_ref[0], split_ref[1]), gram_ref[0])
    out_ref[slot] = by_turn(current_ref[:, columns] - taken, owners)
    send(step, slot).start()
    for s in range(part // LANES):
        tile = before // LANES + step * (part // LANES) + s

        @pl.when(tile // 2 == place_ref[0])
        def _():
            at = pl.ds(pl.multiple_of(lax.rem(tile, 2) * LANES, LANES), LANES)
            gram = gram_ref[0, :, s * LANES : (s + 1) * LANES]
            top_ref[:, at] = dot(inverse_ref[...], gram, ((1,), (0,))) * scale

    @pl.when(step == steps - 1)
    def _():
        send(step - 1, 1 - slot).wait()
        send(step, slot).wait()


def eliminate(scale, me_blk, owners, current, weights, inverse, corner, rest):
    rows, width = current.shape
    wide = width // owners
    groups, n, lanes = corner.shape
    part = rest.shape[2]
    before = groups * lanes

    def whole(*shape):
        return pl.BlockSpec(shape, lambda s, p: (0,) * len(shape))

    out_shape = [
        jax.ShapeDtypeStruct((rows, width), jnp.float32),
        jax.ShapeDtypeStruct((n, wide), jnp.float32),
    ]
    columns = pl.BlockSpec((rows, wide), lambda s, p: (0, s))
    trailing, top = pl.pallas_call(
        functools.partial(lead_kernel, scale, owners),
        grid_spec=pltpu.PrefetchScalarGridSpec(
            num_scalar_prefetch=1,
            grid=(before // wide,),
            in_specs=[
                columns,
                whole(rows, n),
                whole(n, n),
                pl.BlockSpec((wide // lanes, n, lanes), lambda s, p: (s, 0, 0)),
            ],
            out_specs=[columns, whole(n, wide)],
        ),
        out_shape=out_shape,
        compiler_params=pltpu.CompilerParams(vmem_limit_bytes=32 * 2**20),
        cost_estimate=pl.CostEstimate(
            flops=6 * rows * n * before, bytes_accessed=8 * 2**20, transcendentals=0
        ),
    )(me_blk.reshape(1), current, weights, inverse, corner)
    return pl.pallas_call(
        functools.partial(rest_kernel, scale, owners, before),
        grid_spec=pltpu.PrefetchScalarGridSpec(
            num_scalar_prefetch=1,
            grid=(groups,),
            in_specs=[
                whole(rows, width),
                whole(rows, n),
                whole(n, n),
                pl.BlockSpec((1, n, part), lambda s, p: (s, 0, 0)),
                whole(n, wide),
                pl.BlockSpec(memory_space=pl.ANY),
            ],
            out_specs=[pl.BlockSpec(memory_space=pl.ANY), whole(n, wide)],
            scratch_shapes=[
                pltpu.VMEM((2, rows, n), jnp.bfloat16),
                pltpu.VMEM((2, rows, part), jnp.float32),
                pltpu.SemaphoreType.DMA((2,)),
            ],
        ),
        out_shape=out_shape,
        input_output_aliases={6: 0},
        compiler_params=pltpu.CompilerParams(vmem_limit_bytes=40 * 2**20),
        cost_estimate=pl.CostEstimate(
            flops=6 * rows * n * (width - before), bytes_accessed=16 * 2**20, transcendentals=0
        ),
    )(me_blk.reshape(1), current, weights, inverse, rest, top, trailing)


def body(matrix, signs, tile_rows, tile_owner):
    rows_dev, width = matrix.shape
    groups = lax.axis_size("grp")
    owners = lax.axis_size("blk")
    me = lax.axis_index("grp")
    me_blk = lax.axis_index("blk")
    zed, core = me // 2, me % 2
    quads = groups // 2
    tiles = tile_owner.shape[1]
    per_source = TILE // owners
    picked = tiles * per_source
    part = width // groups

    pieces = split_columns(zed, matrix, signs, quads, 0, LANES)
    first = exchange(pieces, core)

    wanted = tile_rows[0].reshape(tiles, per_source, owners)
    selector = jnp.arange(owners, dtype=jnp.int32) == me_blk
    wanted = jnp.sum(jnp.where(selector, wanted, 0), axis=2).reshape(1, picked)
    wanted, *_ = lax.optimization_barrier((wanted, *pieces))
    lists = jnp.concatenate([swap(wanted, "grp", 2 * d) if d else wanted for d in range(quads)])
    lists = jnp.stack([lists, swap(lists, "grp", 1)], axis=1).reshape(groups, picked)
    group = jnp.arange(groups, dtype=jnp.int32)
    lists = jnp.take(lists, group ^ me, axis=0)
    index = jnp.arange(rows_dev, dtype=jnp.int32)
    odd = parity(jnp.maximum(lists, 0)[:, :, None] & index) + parity(group & me)[:, None, None]
    select = jnp.where((lists >= 0)[:, :, None], 1 - 2 * (odd % 2), 0).astype(jnp.bfloat16)
    later = exchange(split_columns(zed, matrix, signs, quads, groups * LANES, part - LANES), core)
    (lead,) = sample(me, select, *first)

    flat = lead.reshape(groups * picked, LANES)
    leads = []
    for d in range(quads):
        mine = swap(flat, "grp", 2 * d) if d else flat
        leads += [mine, swap(mine, "grp", 1)]
    sampled, *backs = sample(me, select, *later, early=lead)
    partial = gram_part(me, sampled.reshape(groups * picked, part), leads)

    share = WIDE // owners
    partial = partial.reshape(owners, share, part)
    summands = lax.all_to_all(partial, "blk", 0, 0, tiled=True)
    backs = [swap(backs[d], "grp", 2 * d) if d else backs[d] for d in range(quads)]
    give = jnp.stack([lax.dynamic_index_in_dim(x, 1 - core, 0, keepdims=False) for x in backs])
    give = swap(give, "grp", 1)
    owner_list = tile_owner[0]
    same = owner_list[:, None] == owner_list[None, :]
    order = jnp.arange(tiles, dtype=jnp.int32)
    rank = jnp.sum((same & (order[None, :] < order[:, None])).astype(jnp.int32), axis=1)
    place = owner_list * MAXT + rank
    hit = place[None, :] == jnp.arange(owners * MAXT, dtype=jnp.int32)[:, None]
    tile_of = jnp.max(jnp.where(hit, order[None, :], -1), axis=1)
    outgoing = pack(me, tile_of, backs, give, per_source)
    outgoing = outgoing.reshape(owners, MAXT * per_source, width)
    outgoing, summands = lax.optimization_barrier((outgoing, summands))
    gram = jnp.sum(summands, axis=0)
    rest = lax.all_gather(gram[:, LANES:], ("grp", "blk"), tiled=True)
    rest = rest.reshape(groups, WIDE, part - LANES)
    corner = gram[:, :LANES][None]
    for axis, strides in (("blk", (1, 2, 3)), ("blk", (4, 8, 12)), ("grp", (2, 4, 6))):
        corner = jnp.stack([corner] + [swap(corner, axis, d) for d in strides])
        corner = corner.reshape(-1, share, LANES)
    corner = corner.reshape(quads, owners, share, LANES)
    inverse, corner = inverse_of_factor(jnp.stack([me, me_blk]), corner, swap(corner, "grp", 1))

    current = lax.all_to_all(outgoing, "blk", 0, 0, tiled=True)
    current = current.reshape(MAXT * TILE, width)

    basis = dot(current[:, :WIDE], inverse, ((1,), (1,)))
    weights = dot(basis, inverse, ((1,), (0,)))
    scale = 1.0 / math.sqrt(groups * owners * TILE)
    trailing, top = eliminate(scale, me_blk, owners, current, weights, inverse, corner, rest)
    return (top, trailing)


def solution(mesh):
    in_specs = (P(("grp", "blk"), None), P(("grp", "blk")), P("grp", None, None), P("grp", None))
    out_specs = (P(None, "blk"), P(("grp", "blk"), None))
    return jax.shard_map(body, mesh=mesh, in_specs=in_specs, out_specs=out_specs, check_vma=False)
```

```python
import functools
import math

import jax
import jax.numpy as jnp
from jax import lax
from jax.experimental import pallas as pl
from jax.experimental.pallas import tpu as pltpu
from jax.sharding import PartitionSpec as P

TILE = 128
MAXT = 2
PANEL = 128
NPAN = 6
WIDE = PANEL * NPAN
LANES = 128
HI = lax.Precision.HIGHEST


def dot(a, b, dims, precision=HI):
    return lax.dot_general(
        a, b, (dims, ((), ())), precision=precision, preferred_element_type=jnp.float32
    )


def inverse_factor(block):
    n = block.shape[0]
    sub = lax.broadcasted_iota(jnp.int32, (n, n), 0)
    lane = lax.broadcasted_iota(jnp.int32, (n, n), 1)
    sub8 = lax.broadcasted_iota(jnp.int32, (8, n), 0)
    left, right = block, (sub == lane).astype(jnp.float32)
    rows = []
    for step in range(n // 8):
        base = 8 * step
        top_left, top_right = left[:8], right[:8]
        cols = [jnp.broadcast_to(top_left[:, base + k : base + k + 1], (8, n)) for k in range(8)]
        pivots = jnp.zeros((8, n), jnp.float32)
        for j in range(8):
            pivot = jnp.broadcast_to(cols[j][j : j + 1], (8, n))
            pivots = jnp.where(sub8 == j, pivot, pivots)
            if j == 7:
                break
            factor = jnp.where(sub8 > j, cols[j] * (1.0 / pivot), 0.0)
            for k in range(j + 1, 8):
                cols[k] = cols[k] - factor * cols[k][j : j + 1]
            top_left = top_left - factor * top_left[j : j + 1]
            top_right = top_right - factor * top_right[j : j + 1]
        scale = lax.rsqrt(pivots)
        top_left, top_right = top_left * scale, top_right * scale
        rows.append(top_right)
        if step < n // 8 - 1:
            turned = top_left.T
            left, right = left[8:], right[8:]
            for k in range(8):
                col = turned[base + 8 :, k : k + 1]
                left = left - col * top_left[k : k + 1]
                right = right - col * top_right[k : k + 1]
    return jnp.concatenate(rows, axis=0)


def factor_kernel(place_ref, own_ref, other_ref, inv_ref, corner_ref, work_ref):
    me, me_blk = place_ref[0], place_ref[1]
    quads, owners, share, lanes = own_ref.shape
    n = owners * share
    for tile in range(2 * quads):
        far = me ^ tile
        for owner in range(owners):
            rows = slice(owner * share, (owner + 1) * share)
            near = me_blk ^ owner
            piece = jnp.where(far % 2 == 0, own_ref[far // 2, near], other_ref[far // 2, near])
            corner_ref[tile, rows, :] = piece
            if tile * lanes < n:
                work_ref[rows, tile * lanes : (tile + 1) * lanes] = piece
    inv_ref[...] = jnp.zeros_like(inv_ref)
    for low in range(0, n, PANEL):
        high = low + PANEL
        inverse = inverse_factor(work_ref[low:high, low:high])
        inv_ref[low:high, low:high] = inverse
        if low:
            inv_ref[low:high, :low] = dot(inverse, inv_ref[low:high, :low], ((1,), (0,)))
        if high < n:
            upper = dot(inverse, work_ref[low:high, high:], ((1,), (0,)))
            work_ref[high:, high:] -= dot(upper, upper, ((0,), (0,)))
            inv_ref[high:, :high] -= dot(upper, inv_ref[low:high, :high], ((0,), (0,)))


def inverse_of_factor(place, own, other):
    quads, owners, share, lanes = own.shape
    n = owners * share
    return pl.pallas_call(
        factor_kernel,
        out_shape=(
            jax.ShapeDtypeStruct((n, n), jnp.float32),
            jax.ShapeDtypeStruct((2 * quads, n, lanes), jnp.float32),
        ),
        in_specs=[pl.BlockSpec(memory_space=pltpu.SMEM)]
        + [pl.BlockSpec(memory_space=pltpu.VMEM)] * 2,
        out_specs=(pl.BlockSpec(memory_space=pltpu.VMEM), pl.BlockSpec(memory_space=pltpu.VMEM)),
        scratch_shapes=[pltpu.VMEM((n, n), jnp.float32)],
        compiler_params=pltpu.CompilerParams(vmem_limit_bytes=32 * 2**20),
        cost_estimate=pl.CostEstimate(
            flops=10**9, bytes_accessed=6 * 2**20, transcendentals=0
        ),
    )(place, own, other)


def swap(x, axis, d):
    return lax.ppermute(x, axis, [(i, i ^ d) for i in range(lax.axis_size(axis))])


def exchange(pieces, core):
    kept = [swap(x, "grp", 2 * d) if d else x for d, x in enumerate(pieces)]
    other = [lax.dynamic_index_in_dim(x, 1 - core, 0, keepdims=False) for x in kept]
    return kept, [swap(x, "grp", 1) for x in other]


def parity(x):
    return lax.population_count(x) % 2


def split_kernel(quads, per, place_ref, sign_ref, *refs):
    sources, outs = refs[: quads * per], refs[quads * per :]
    sign = sign_ref[...].astype(jnp.float32)
    for d, out in enumerate(outs):
        half = out.shape[2]
        for s, source in enumerate(sources[d * per : (d + 1) * per]):
            signed = source[...] * sign
            for part in range(2):
                core, at = divmod((2 * s + part) * LANES, half)
                out[core, :, at : at + LANES] = signed[:, part * LANES : (part + 1) * LANES]


def split_columns(zed, matrix, signs, quads, first, part):
    rows = matrix.shape[0]
    block = 2 * LANES
    per = 2 * part // block
    reads = [
        pl.BlockSpec(
            (rows, block), lambda i, z, d=d, s=s: (0, first // block + (z[0] ^ d) * per + s)
        )
        for d in range(quads)
        for s in range(per)
    ]
    shape = (2, rows, part)
    return pl.pallas_call(
        functools.partial(split_kernel, quads, per),
        grid_spec=pltpu.PrefetchScalarGridSpec(
            num_scalar_prefetch=1,
            grid=(1,),
            in_specs=[pl.BlockSpec((rows, 1), lambda i, z: (0, 0))] + reads,
            out_specs=[pl.BlockSpec(shape, lambda i, z: (0, 0, 0))] * quads,
        ),
        out_shape=[jax.ShapeDtypeStruct(shape, jnp.float32)] * quads,
        compiler_params=pltpu.CompilerParams(vmem_limit_bytes=32 * 2**20),
        cost_estimate=pl.CostEstimate(
            flops=2 * quads * rows * part,
            bytes_accessed=16 * quads * rows * part,
            transcendentals=0,
        ),
    )(zed.reshape(1), signs.reshape(rows, 1), *[matrix] * (quads * per))


def sample_kernel(scale, quads, has_early, place_ref, select_ref, *refs):
    mixed_ref = refs[-1]
    groups, rows, width = mixed_ref.shape
    kept, given = refs[:quads], refs[quads : 2 * quads]
    early_ref = refs[2 * quads] if has_early else None
    sampled_ref = refs[2 * quads + has_early]
    backs = refs[2 * quads + has_early + 1 : -1]
    step = 16 if width <= 128 else 8

    def mix(r, carry):
        at = pl.ds(pl.multiple_of(r * step, step), step)
        parts = []
        for d in range(quads):
            parts += [kept[d][0, at, :], given[d][at, :]]
        level = 1
        while level < groups:
            new = list(parts)
            for k in range(groups):
                if not k & level:
                    new[k] = parts[k] + parts[k | level]
                    new[k | level] = parts[k] - parts[k | level]
            parts = new
            level *= 2
        for k in range(groups):
            mixed_ref[k, at, :] = parts[k]
        return carry

    lax.fori_loop(0, rows // step, mix, 0)
    zed = place_ref[0] // 2
    for d in range(quads):
        for c in range(2):
            group = 2 * (zed ^ d) + c
            left = select_ref[group]
            value = mixed_ref[group]
            total = None
            for _ in range(3):
                high = value.astype(jnp.bfloat16)
                term = jnp.dot(left, high, preferred_element_type=jnp.float32)
                total = term if total is None else total + term
                value = value - high.astype(jnp.float32)
            total = total * scale
            if early_ref is None:
                sampled_ref[group] = total
                continue
            early = early_ref[group]
            done = early.shape[1]
            sampled_ref[group, :, :done] = early
            sampled_ref[group, :, done:] = total
            backs[d][c, :, :done] = early
            backs[d][c, :, done:] = total


def sample(me, select, kept, given, early=None):
    groups, picked, rows = select.shape
    quads = groups // 2
    block = given[0].shape[1]

    def whole(*shape):
        return pl.BlockSpec(shape, lambda s, p: (0,) * len(shape))

    in_specs = [whole(groups, picked, rows)]
    in_specs += [pl.BlockSpec((1, rows, block), lambda s, p: (p[0] % 2, 0, 0))] * quads
    in_specs += [whole(rows, block)] * quads
    shapes = [(groups, picked, block)]
    if early is not None:
        in_specs.append(whole(*early.shape))
        part = block + early.shape[2]
        shapes = [(groups, picked, part)] + [(2, picked, part)] * quads
    return pl.pallas_call(
        functools.partial(
            sample_kernel, 1.0 / math.sqrt(groups * rows), quads, early is not None
        ),
        grid_spec=pltpu.PrefetchScalarGridSpec(
            num_scalar_prefetch=1,
            grid=(1,),
            in_specs=in_specs,
            out_specs=[whole(*shape) for shape in shapes],
            scratch_shapes=[pltpu.VMEM((groups, rows, block), jnp.float32)],
        ),
        out_shape=[jax.ShapeDtypeStruct(shape, jnp.float32) for shape in shapes],
        compiler_params=pltpu.CompilerParams(vmem_limit_bytes=40 * 2**20),
        cost_estimate=pl.CostEstimate(
            flops=6 * groups * picked * rows * block, bytes_accessed=9 * 2**20, transcendentals=0
        ),
    )(me.reshape(1), select, *kept, *given, *([] if early is None else [early]))


def gram_kernel(place_ref, rest_ref, *refs):
    leads, out_ref, all_ref = refs[:-2], refs[-2], refs[-1]
    for k, lead in enumerate(leads):
        tile = place_ref[0] ^ k

        @pl.when(tile < NPAN)
        def _():
            at = pl.ds(pl.multiple_of(tile * LANES, LANES), LANES)
            all_ref[:, at] = lead[...]

    out_ref[...] = dot(all_ref[...], rest_ref[...], ((0,), (0,)))


def gram_part(me, rest, leads):
    rows, part = rest.shape
    return pl.pallas_call(
        gram_kernel,
        out_shape=jax.ShapeDtypeStruct((WIDE, part), jnp.float32),
        in_specs=[pl.BlockSpec(memory_space=pltpu.SMEM)]
        + [pl.BlockSpec(memory_space=pltpu.VMEM)] * (1 + len(leads)),
        out_specs=pl.BlockSpec(memory_space=pltpu.VMEM),
        scratch_shapes=[pltpu.VMEM((rows, WIDE), jnp.float32)],
        compiler_params=pltpu.CompilerParams(vmem_limit_bytes=36 * 2**20),
        cost_estimate=pl.CostEstimate(
            flops=12 * rows * WIDE * part, bytes_accessed=8 * 2**20, transcendentals=0
        ),
    )(me.reshape(1), rest, *leads)


def pack_kernel(place_ref, tile_ref, *refs):
    out_ref, given_ref = refs[-1], refs[-2]
    kept = refs[:-2]
    quads = len(kept)
    places, per, width = out_ref.shape
    groups = 2 * quads
    rest = width // groups - LANES
    me = place_ref[0]

    def fill(q, carry):
        tile = tile_ref[q]
        at = pl.ds(pl.multiple_of(jnp.maximum(tile, 0) * per, per), per)
        for d in range(quads):
            for e in range(2):
                rows = given_ref[d, at, :] if e else kept[d][0, at, :]
                rows = jnp.where(tile >= 0, rows, 0.0)
                far = me ^ (2 * d + e)
                where = pl.ds(pl.multiple_of(far * LANES, LANES), LANES)
                out_ref[q, :, where] = rows[:, :LANES]
                column = groups * LANES + far * rest
                where = pl.ds(pl.multiple_of(column, LANES), rest)
                out_ref[q, :, where] = rows[:, LANES:]
        return carry

    lax.fori_loop(0, places, fill, 0)


def pack(me, tile_of, kept, given, per):
    places = tile_of.shape[0]
    quads, picked, part = given.shape
    width = 2 * quads * part
    whole = (quads, picked, part)
    return pl.pallas_call(
        pack_kernel,
        grid_spec=pltpu.PrefetchScalarGridSpec(
            num_scalar_prefetch=2,
            grid=(1,),
            in_specs=[pl.BlockSpec((1, picked, part), lambda s, p, t: (p[0] % 2, 0, 0))] * quads
            + [pl.BlockSpec(whole, lambda s, p, t: (0, 0, 0))],
            out_specs=pl.BlockSpec((places, per, width), lambda s, p, t: (0, 0, 0)),
        ),
        out_shape=jax.ShapeDtypeStruct((places, per, width), jnp.float32),
        compiler_params=pltpu.CompilerParams(vmem_limit_bytes=32 * 2**20),
        cost_estimate=pl.CostEstimate(flops=0, bytes_accessed=8 * 2**20, transcendentals=0),
    )(me.reshape(1), tile_of, *kept, given)


def halves(x):
    high = x.astype(jnp.bfloat16)
    return high, (x - high.astype(jnp.float32)).astype(jnp.bfloat16)


def product(weights, gram):
    high, low = halves(gram)

    def term(a, b):
        return jnp.dot(a, b, preferred_element_type=jnp.float32)

    return term(weights[0], high) + (term(weights[0], low) + term(weights[1], high))


def by_turn(value, owners):
    rows, columns = value.shape
    value = value.reshape(owners, rows // owners, columns)
    return jnp.swapaxes(value, 0, 1).reshape(rows, columns)


def lead_kernel(
    scale, owners, place_ref, current_ref, weights_ref, inverse_ref, gram_ref, trailing_ref, top_ref
):
    step = pl.program_id(0)
    gram = jnp.concatenate([gram_ref[0], gram_ref[1]], axis=1)
    taken = product(halves(weights_ref[...]), gram)
    trailing_ref[...] = by_turn(current_ref[...] - taken, owners)

    @pl.when(step == 0)
    def _():
        top_ref[...] = jnp.zeros_like(top_ref)

    @pl.when(step == place_ref[0])
    def _():
        top = dot(inverse_ref[...], gram, ((1,), (0,)))
        row = lax.broadcasted_iota(jnp.int32, top.shape, 0)
        column = lax.broadcasted_iota(jnp.int32, top.shape, 1) + step * top.shape[1]
        top_ref[...] = jnp.where(column >= row // PANEL * PANEL, top, 0.0) * scale


def rest_kernel(
    scale, owners, before, place_ref, current_ref, weights_ref, inverse_ref, gram_ref, lead_ref,
    trailing_in, trailing_ref, top_ref, split_ref, out_ref, sems
):
    step, steps = pl.program_id(0), pl.num_programs(0)
    part = gram_ref.shape[2]
    slot = lax.rem(step, 2)

    def send(step, slot):
        columns = pl.ds(pl.multiple_of(before + step * part, LANES), part)
        return pltpu.make_async_copy(out_ref.at[slot], trailing_ref.at[:, columns], sems.at[slot])

    @pl.when(step == 0)
    def _():
        split_ref[0], split_ref[1] = halves(weights_ref[...])
        top_ref[...] = lead_ref[...]

    @pl.when(step >= 2)
    def _():
        send(step - 2, slot).wait()

    columns = pl.ds(pl.multiple_of(before + step * part, LANES), part)
    taken = product((split_ref[0], split_ref[1]), gram_ref[0])
    out_ref[slot] = by_turn(current_ref[:, columns] - taken, owners)
    send(step, slot).start()
    for s in range(part // LANES):
        tile = before // LANES + step * (part // LANES) + s

        @pl.when(tile // 2 == place_ref[0])
        def _():
            at = pl.ds(pl.multiple_of(lax.rem(tile, 2) * LANES, LANES), LANES)
            gram = gram_ref[0, :, s * LANES : (s + 1) * LANES]
            top_ref[:, at] = dot(inverse_ref[...], gram, ((1,), (0,))) * scale

    @pl.when(step == steps - 1)
    def _():
        send(step - 1, 1 - slot).wait()
        send(step, slot).wait()


def eliminate(scale, me_blk, owners, current, weights, inverse, corner, rest):
    rows, width = current.shape
    wide = width // owners
    groups, n, lanes = corner.shape
    part = rest.shape[2]
    before = groups * lanes

    def whole(*shape):
        return pl.BlockSpec(shape, lambda s, p: (0,) * len(shape))

    out_shape = [
        jax.ShapeDtypeStruct((rows, width), jnp.float32),
        jax.ShapeDtypeStruct((n, wide), jnp.float32),
    ]
    held = pl.BlockSpec(memory_space=pltpu.VMEM)
    columns = pl.BlockSpec((rows, wide), lambda s, p: (0, s))
    trailing, top = pl.pallas_call(
        functools.partial(lead_kernel, scale, owners),
        grid_spec=pltpu.PrefetchScalarGridSpec(
            num_scalar_prefetch=1,
            grid=(before // wide,),
            in_specs=[
                columns,
                held,
                held,
                pl.BlockSpec((wide // lanes, n, lanes), lambda s, p: (s, 0, 0)),
            ],
            out_specs=[columns, whole(n, wide)],
        ),
        out_shape=out_shape,
        compiler_params=pltpu.CompilerParams(vmem_limit_bytes=20 * 2**20),
        cost_estimate=pl.CostEstimate(
            flops=6 * rows * n * before, bytes_accessed=8 * 2**20, transcendentals=0
        ),
    )(me_blk.reshape(1), current, weights, inverse, corner)
    return pl.pallas_call(
        functools.partial(rest_kernel, scale, owners, before),
        grid_spec=pltpu.PrefetchScalarGridSpec(
            num_scalar_prefetch=1,
            grid=(groups,),
            in_specs=[
                held,
                held,
                held,
                pl.BlockSpec((1, n, part), lambda s, p: (s, 0, 0)),
                held,
                pl.BlockSpec(memory_space=pl.ANY),
            ],
            out_specs=[pl.BlockSpec(memory_space=pl.ANY), whole(n, wide)],
            scratch_shapes=[
                pltpu.VMEM((2, rows, n), jnp.bfloat16),
                pltpu.VMEM((2, rows, part), jnp.float32),
                pltpu.SemaphoreType.DMA((2,)),
            ],
        ),
        out_shape=out_shape,
        input_output_aliases={6: 0},
        compiler_params=pltpu.CompilerParams(vmem_limit_bytes=44 * 2**20),
        cost_estimate=pl.CostEstimate(
            flops=6 * rows * n * (width - before), bytes_accessed=16 * 2**20, transcendentals=0
        ),
    )(me_blk.reshape(1), current, weights, inverse, rest, top, trailing)


def body(matrix, signs, tile_rows, tile_owner):
    rows_dev, width = matrix.shape
    groups = lax.axis_size("grp")
    owners = lax.axis_size("blk")
    me = lax.axis_index("grp")
    me_blk = lax.axis_index("blk")
    zed, core = me // 2, me % 2
    quads = groups // 2
    tiles = tile_owner.shape[1]
    per_source = TILE // owners
    picked = tiles * per_source
    part = width // groups

    pieces = split_columns(zed, matrix, signs, quads, 0, LANES)
    first = exchange(pieces, core)

    wanted = tile_rows[0].reshape(tiles, per_source, owners)
    selector = jnp.arange(owners, dtype=jnp.int32) == me_blk
    wanted = jnp.sum(jnp.where(selector, wanted, 0), axis=2).reshape(1, picked)
    wanted, *_ = lax.optimization_barrier((wanted, *pieces))
    lists = jnp.concatenate([swap(wanted, "grp", 2 * d) if d else wanted for d in range(quads)])
    lists = jnp.stack([lists, swap(lists, "grp", 1)], axis=1).reshape(groups, picked)
    group = jnp.arange(groups, dtype=jnp.int32)
    lists = jnp.take(lists, group ^ me, axis=0)
    index = jnp.arange(rows_dev, dtype=jnp.int32)
    odd = parity(jnp.maximum(lists, 0)[:, :, None] & index) + parity(group & me)[:, None, None]
    select = jnp.where((lists >= 0)[:, :, None], 1 - 2 * (odd % 2), 0).astype(jnp.bfloat16)
    later = exchange(split_columns(zed, matrix, signs, quads, groups * LANES, part - LANES), core)
    (lead,) = sample(me, select, *first)

    flat = lead.reshape(groups * picked, LANES)
    leads = []
    for d in range(quads):
        mine = swap(flat, "grp", 2 * d) if d else flat
        leads += [mine, swap(mine, "grp", 1)]
    sampled, *backs = sample(me, select, *later, early=lead)
    partial = gram_part(me, sampled.reshape(groups * picked, part), leads)

    share = WIDE // owners
    partial = partial.reshape(owners, share, part)
    partial, *backs = lax.optimization_barrier((partial, *backs))
    summands = lax.all_to_all(partial, "blk", 0, 0, tiled=True)
    backs = [swap(backs[d], "grp", 2 * d) if d else backs[d] for d in range(quads)]
    give = jnp.stack([lax.dynamic_index_in_dim(x, 1 - core, 0, keepdims=False) for x in backs])
    give = swap(give, "grp", 1)
    owner_list = tile_owner[0]
    same = owner_list[:, None] == owner_list[None, :]
    order = jnp.arange(tiles, dtype=jnp.int32)
    rank = jnp.sum((same & (order[None, :] < order[:, None])).astype(jnp.int32), axis=1)
    place = owner_list * MAXT + rank
    hit = place[None, :] == jnp.arange(owners * MAXT, dtype=jnp.int32)[:, None]
    tile_of = jnp.max(jnp.where(hit, order[None, :], -1), axis=1)
    outgoing = pack(me, tile_of, backs, give, per_source)
    outgoing = outgoing.reshape(owners, MAXT * per_source, width)
    outgoing, summands = lax.optimization_barrier((outgoing, summands))
    gram = jnp.sum(summands, axis=0)
    rest = lax.all_gather(gram[:, LANES:], ("grp", "blk"), tiled=True)
    rest = rest.reshape(groups, WIDE, part - LANES)
    corner = gram[:, :LANES][None]
    for axis, strides in (("blk", (1, 2, 3)), ("blk", (4, 8, 12)), ("grp", (2, 4, 6))):
        corner = jnp.stack([corner] + [swap(corner, axis, d) for d in strides])
        corner = corner.reshape(-1, share, LANES)
        if strides == (4, 8, 12):
            corner, outgoing = lax.optimization_barrier((corner, outgoing))
    corner = corner.reshape(quads, owners, share, LANES)
    inverse, corner = inverse_of_factor(jnp.stack([me, me_blk]), corner, swap(corner, "grp", 1))

    current = lax.all_to_all(outgoing, "blk", 0, 0, tiled=True)
    current = current.reshape(MAXT * TILE, width)

    basis = dot(current[:, :WIDE], inverse, ((1,), (1,)))
    weights = dot(basis, inverse, ((1,), (0,)))
    scale = 1.0 / math.sqrt(groups * owners * TILE)
    trailing, top = eliminate(scale, me_blk, owners, current, weights, inverse, corner, rest)
    return (top, trailing)


def solution(mesh):
    in_specs = (P(("grp", "blk"), None), P(("grp", "blk")), P("grp", None, None), P("grp", None))
    out_specs = (P(None, "blk"), P(("grp", "blk"), None))
    return jax.shard_map(body, mesh=mesh, in_specs=in_specs, out_specs=out_specs, check_vma=False)
```

```python
import functools
import math

import jax
import jax.numpy as jnp
from jax import lax
from jax.experimental import pallas as pl
from jax.experimental.pallas import tpu as pltpu
from jax.sharding import PartitionSpec as P

TILE = 128
MAXT = 2
PANEL = 128
NPAN = 6
WIDE = PANEL * NPAN
LANES = 128
HI = lax.Precision.HIGHEST


def dot(a, b, dims, precision=HI):
    return lax.dot_general(
        a, b, (dims, ((), ())), precision=precision, preferred_element_type=jnp.float32
    )


def inverse_factor(block):
    n = block.shape[0]
    sub = lax.broadcasted_iota(jnp.int32, (n, n), 0)
    lane = lax.broadcasted_iota(jnp.int32, (n, n), 1)
    sub8 = lax.broadcasted_iota(jnp.int32, (8, n), 0)
    left, right = block, (sub == lane).astype(jnp.float32)
    rows = []
    for step in range(n // 8):
        base = 8 * step
        top_left, top_right = left[:8], right[:8]
        cols = [jnp.broadcast_to(top_left[:, base + k : base + k + 1], (8, n)) for k in range(8)]
        pivots = jnp.zeros((8, n), jnp.float32)
        for j in range(8):
            pivot = jnp.broadcast_to(cols[j][j : j + 1], (8, n))
            pivots = jnp.where(sub8 == j, pivot, pivots)
            if j == 7:
                break
            factor = jnp.where(sub8 > j, cols[j] * (1.0 / pivot), 0.0)
            for k in range(j + 1, 8):
                cols[k] = cols[k] - factor * cols[k][j : j + 1]
            top_left = top_left - factor * top_left[j : j + 1]
            top_right = top_right - factor * top_right[j : j + 1]
        scale = lax.rsqrt(pivots)
        top_left, top_right = top_left * scale, top_right * scale
        rows.append(top_right)
        if step < n // 8 - 1:
            turned = top_left.T
            left, right = left[8:], right[8:]
            for k in range(8):
                col = turned[base + 8 :, k : k + 1]
                left = left - col * top_left[k : k + 1]
                right = right - col * top_right[k : k + 1]
    return jnp.concatenate(rows, axis=0)


def factor_kernel(place_ref, own_ref, other_ref, inv_ref, corner_ref, work_ref):
    me, me_blk = place_ref[0], place_ref[1]
    quads, owners, share, lanes = own_ref.shape
    n = owners * share
    for tile in range(2 * quads):
        far = me ^ tile
        for owner in range(owners):
            rows = slice(owner * share, (owner + 1) * share)
            near = me_blk ^ owner
            piece = jnp.where(far % 2 == 0, own_ref[far // 2, near], other_ref[far // 2, near])
            corner_ref[tile, rows, :] = piece
            if tile * lanes < n:
                work_ref[rows, tile * lanes : (tile + 1) * lanes] = piece
    inv_ref[...] = jnp.zeros_like(inv_ref)
    for low in range(0, n, PANEL):
        high = low + PANEL
        inverse = inverse_factor(work_ref[low:high, low:high])
        inv_ref[low:high, low:high] = inverse
        if low:
            inv_ref[low:high, :low] = dot(inverse, inv_ref[low:high, :low], ((1,), (0,)))
        if high < n:
            upper = dot(inverse, work_ref[low:high, high:], ((1,), (0,)))
            work_ref[high:, high:] -= dot(upper, upper, ((0,), (0,)))
            inv_ref[high:, :high] -= dot(upper, inv_ref[low:high, :high], ((0,), (0,)))


def inverse_of_factor(place, own, other):
    quads, owners, share, lanes = own.shape
    n = owners * share
    return pl.pallas_call(
        factor_kernel,
        out_shape=(
            jax.ShapeDtypeStruct((n, n), jnp.float32),
            jax.ShapeDtypeStruct((2 * quads, n, lanes), jnp.float32),
        ),
        in_specs=[pl.BlockSpec(memory_space=pltpu.SMEM)]
        + [pl.BlockSpec(memory_space=pltpu.VMEM)] * 2,
        out_specs=(pl.BlockSpec(memory_space=pltpu.VMEM), pl.BlockSpec(memory_space=pltpu.VMEM)),
        scratch_shapes=[pltpu.VMEM((n, n), jnp.float32)],
        compiler_params=pltpu.CompilerParams(vmem_limit_bytes=32 * 2**20),
        cost_estimate=pl.CostEstimate(
            flops=10**9, bytes_accessed=6 * 2**20, transcendentals=0
        ),
    )(place, own, other)


def swap(x, axis, d):
    return lax.ppermute(x, axis, [(i, i ^ d) for i in range(lax.axis_size(axis))])


def exchange(pieces, core):
    kept = [swap(x, "grp", 2 * d) if d else x for d, x in enumerate(pieces)]
    other = [lax.dynamic_index_in_dim(x, 1 - core, 0, keepdims=False) for x in kept]
    return kept, [swap(x, "grp", 1) for x in other]


def parity(x):
    for shift in (4, 2, 1):
        x = x ^ lax.shift_right_logical(x, shift)
    return x & 1


def split_kernel(quads, per, place_ref, sign_ref, extra_ref, *refs):
    sources, outs = refs[: quads * per], refs[quads * per :]
    rows = sign_ref.shape[0]
    sign = sign_ref[...].astype(jnp.float32)
    for d, out in enumerate(outs):
        half = out.shape[2]
        for s, source in enumerate(sources[d * per : (d + 1) * per]):
            signed = source[...] * sign
            for part in range(2):
                core, at = divmod((2 * s + part) * LANES, half)
                out[core, :rows, at : at + LANES] = signed[:, part * LANES : (part + 1) * LANES]
        if out.shape[1] > rows:
            out[0, rows:, :] = extra_ref[...]
            out[1, rows:, :] = extra_ref[...]


def split_columns(zed, matrix, signs, extra, quads, first, part):
    rows = matrix.shape[0]
    block = 2 * LANES
    per = 2 * part // block
    reads = [
        pl.BlockSpec(
            (rows, block), lambda i, z, d=d, s=s: (0, first // block + (z[0] ^ d) * per + s)
        )
        for d in range(quads)
        for s in range(per)
    ]
    shape = (2, rows + (8 if extra.shape[1] == part else 0), part)
    return pl.pallas_call(
        functools.partial(split_kernel, quads, per),
        grid_spec=pltpu.PrefetchScalarGridSpec(
            num_scalar_prefetch=1,
            grid=(1,),
            in_specs=[pl.BlockSpec((rows, 1), lambda i, z: (0, 0))]
            + [pl.BlockSpec(extra.shape, lambda i, z: (0, 0))]
            + reads,
            out_specs=[pl.BlockSpec(shape, lambda i, z: (0, 0, 0))] * quads,
        ),
        out_shape=[jax.ShapeDtypeStruct(shape, jnp.float32)] * quads,
        compiler_params=pltpu.CompilerParams(vmem_limit_bytes=32 * 2**20),
        cost_estimate=pl.CostEstimate(
            flops=2 * quads * rows * part,
            bytes_accessed=16 * quads * rows * part,
            transcendentals=0,
        ),
    )(zed.reshape(1), signs.reshape(rows, 1), extra, *[matrix] * (quads * per))


def sample_first_kernel(scale, quads, place_ref, *refs):
    kept, given = refs[:quads], refs[quads : 2 * quads]
    sampled_ref, select_ref, mixed_ref = refs[2 * quads :]
    groups, picked, rows = select_ref.shape
    me = place_ref[0]
    column = lax.broadcasted_iota(jnp.int32, (picked, rows), 1)
    for d in range(quads):
        for e in range(2):
            lists = given[d][rows:, :] if e else kept[d][0, rows:, :]
            wanted = lists.T[:, :1].astype(jnp.int32)
            group = me ^ (2 * d + e)
            odd = parity(jnp.maximum(wanted, 0) & column) ^ parity(group & me)
            select = jnp.where(wanted >= 0, 1 - 2 * odd, 0)
            select_ref[group] = select.astype(jnp.float32).astype(jnp.bfloat16)
    sample_kernel(scale, quads, False, place_ref, select_ref, *kept, *given, sampled_ref, mixed_ref)


def sample_first(me, rows, picked, kept, given):
    quads = len(kept)
    groups = 2 * quads
    sent, block = given[0].shape

    def whole(*shape):
        return pl.BlockSpec(shape, lambda s, p: (0,) * len(shape))

    shapes = [(groups, picked, block), (groups, picked, rows)]
    return pl.pallas_call(
        functools.partial(sample_first_kernel, 1.0 / math.sqrt(groups * rows), quads),
        grid_spec=pltpu.PrefetchScalarGridSpec(
            num_scalar_prefetch=1,
            grid=(1,),
            in_specs=[pl.BlockSpec((1, sent, block), lambda s, p: (p[0] % 2, 0, 0))] * quads
            + [whole(sent, block)] * quads,
            out_specs=[whole(*shape) for shape in shapes],
            scratch_shapes=[pltpu.VMEM((groups, rows, block), jnp.float32)],
        ),
        out_shape=[
            jax.ShapeDtypeStruct(shapes[0], jnp.float32),
            jax.ShapeDtypeStruct(shapes[1], jnp.bfloat16),
        ],
        compiler_params=pltpu.CompilerParams(vmem_limit_bytes=24 * 2**20),
        cost_estimate=pl.CostEstimate(
            flops=6 * groups * picked * rows * block, bytes_accessed=4 * 2**20, transcendentals=0
        ),
    )(me.reshape(1), *kept, *given)


def sample_kernel(scale, quads, has_early, place_ref, select_ref, *refs):
    mixed_ref = refs[-1]
    groups, rows, width = mixed_ref.shape
    kept, given = refs[:quads], refs[quads : 2 * quads]
    early_ref = refs[2 * quads] if has_early else None
    sampled_ref = refs[2 * quads + has_early]
    backs = refs[2 * quads + has_early + 1 : -1]
    step = 16 if width <= 128 else 8

    def mix(r, carry):
        at = pl.ds(pl.multiple_of(r * step, step), step)
        parts = []
        for d in range(quads):
            parts += [kept[d][0, at, :], given[d][at, :]]
        level = 1
        while level < groups:
            new = list(parts)
            for k in range(groups):
                if not k & level:
                    new[k] = parts[k] + parts[k | level]
                    new[k | level] = parts[k] - parts[k | level]
            parts = new
            level *= 2
        for k in range(groups):
            mixed_ref[k, at, :] = parts[k]
        return carry

    lax.fori_loop(0, rows // step, mix, 0)
    zed = place_ref[0] // 2
    for d in range(quads):
        for c in range(2):
            group = 2 * (zed ^ d) + c
            left = select_ref[group]
            value = mixed_ref[group]
            total = None
            for _ in range(3):
                high = value.astype(jnp.bfloat16)
                term = jnp.dot(left, high, preferred_element_type=jnp.float32)
                total = term if total is None else total + term
                value = value - high.astype(jnp.float32)
            total = total * scale
            if early_ref is None:
                sampled_ref[group] = total
                continue
            early = early_ref[group]
            done = early.shape[1]
            sampled_ref[group, :, :done] = early
            sampled_ref[group, :, done:] = total
            backs[d][c, :, :done] = early
            backs[d][c, :, done:] = total


def sample(me, select, kept, given, early):
    groups, picked, rows = select.shape
    quads = groups // 2
    block = given[0].shape[1]

    def whole(*shape):
        return pl.BlockSpec(shape, lambda s, p: (0,) * len(shape))

    in_specs = [whole(groups, picked, rows)]
    in_specs += [pl.BlockSpec((1, rows, block), lambda s, p: (p[0] % 2, 0, 0))] * quads
    in_specs += [whole(rows, block)] * quads
    in_specs.append(whole(*early.shape))
    part = block + early.shape[2]
    shapes = [(groups, picked, part)] + [(2, picked, part)] * quads
    return pl.pallas_call(
        functools.partial(sample_kernel, 1.0 / math.sqrt(groups * rows), quads, True),
        grid_spec=pltpu.PrefetchScalarGridSpec(
            num_scalar_prefetch=1,
            grid=(1,),
            in_specs=in_specs,
            out_specs=[whole(*shape) for shape in shapes],
            scratch_shapes=[pltpu.VMEM((groups, rows, block), jnp.float32)],
        ),
        out_shape=[jax.ShapeDtypeStruct(shape, jnp.float32) for shape in shapes],
        compiler_params=pltpu.CompilerParams(vmem_limit_bytes=40 * 2**20),
        cost_estimate=pl.CostEstimate(
            flops=6 * groups * picked * rows * block, bytes_accessed=9 * 2**20, transcendentals=0
        ),
    )(me.reshape(1), select, *kept, *given, early)


def gram_kernel(place_ref, rest_ref, *refs):
    leads, out_ref, all_ref = refs[:-2], refs[-2], refs[-1]
    for k, lead in enumerate(leads):
        tile = place_ref[0] ^ k

        @pl.when(tile < NPAN)
        def _():
            at = pl.ds(pl.multiple_of(tile * LANES, LANES), LANES)
            all_ref[:, at] = lead[...]

    out_ref[...] = dot(all_ref[...], rest_ref[...], ((0,), (0,)))


def gram_part(me, rest, leads):
    rows, part = rest.shape
    return pl.pallas_call(
        gram_kernel,
        out_shape=jax.ShapeDtypeStruct((WIDE, part), jnp.float32),
        in_specs=[pl.BlockSpec(memory_space=pltpu.SMEM)]
        + [pl.BlockSpec(memory_space=pltpu.VMEM)] * (1 + len(leads)),
        out_specs=pl.BlockSpec(memory_space=pltpu.VMEM),
        scratch_shapes=[pltpu.VMEM((rows, WIDE), jnp.float32)],
        compiler_params=pltpu.CompilerParams(vmem_limit_bytes=36 * 2**20),
        cost_estimate=pl.CostEstimate(
            flops=12 * rows * WIDE * part, bytes_accessed=8 * 2**20, transcendentals=0
        ),
    )(me.reshape(1), rest, *leads)


def pack_kernel(place_ref, tile_ref, *refs):
    out_ref, given_ref = refs[-1], refs[-2]
    kept = refs[:-2]
    quads = len(kept)
    places, per, width = out_ref.shape
    groups = 2 * quads
    rest = width // groups - LANES
    me = place_ref[0]

    def fill(q, carry):
        tile = tile_ref[q]
        at = pl.ds(pl.multiple_of(jnp.maximum(tile, 0) * per, per), per)
        for d in range(quads):
            for e in range(2):
                rows = given_ref[d, at, :] if e else kept[d][0, at, :]
                rows = jnp.where(tile >= 0, rows, 0.0)
                far = me ^ (2 * d + e)
                where = pl.ds(pl.multiple_of(far * LANES, LANES), LANES)
                out_ref[q, :, where] = rows[:, :LANES]
                column = groups * LANES + far * rest
                where = pl.ds(pl.multiple_of(column, LANES), rest)
                out_ref[q, :, where] = rows[:, LANES:]
        return carry

    lax.fori_loop(0, places, fill, 0)


def pack(me, tile_of, kept, given, per):
    places = tile_of.shape[0]
    quads, picked, part = given.shape
    width = 2 * quads * part
    whole = (quads, picked, part)
    return pl.pallas_call(
        pack_kernel,
        grid_spec=pltpu.PrefetchScalarGridSpec(
            num_scalar_prefetch=2,
            grid=(1,),
            in_specs=[pl.BlockSpec((1, picked, part), lambda s, p, t: (p[0] % 2, 0, 0))] * quads
            + [pl.BlockSpec(whole, lambda s, p, t: (0, 0, 0))],
            out_specs=pl.BlockSpec((places, per, width), lambda s, p, t: (0, 0, 0)),
        ),
        out_shape=jax.ShapeDtypeStruct((places, per, width), jnp.float32),
        compiler_params=pltpu.CompilerParams(vmem_limit_bytes=32 * 2**20),
        cost_estimate=pl.CostEstimate(flops=0, bytes_accessed=8 * 2**20, transcendentals=0),
    )(me.reshape(1), tile_of, *kept, given)


def halves(x):
    high = x.astype(jnp.bfloat16)
    return high, (x - high.astype(jnp.float32)).astype(jnp.bfloat16)


def product(weights, gram):
    high, low = halves(gram)

    def term(a, b):
        return jnp.dot(a, b, preferred_element_type=jnp.float32)

    return term(weights[0], high) + (term(weights[0], low) + term(weights[1], high))


def by_turn(value, owners):
    rows, columns = value.shape
    value = value.reshape(owners, rows // owners, columns)
    return jnp.swapaxes(value, 0, 1).reshape(rows, columns)


def lead_kernel(
    scale, owners, place_ref, current_ref, weights_ref, inverse_ref, gram_ref, trailing_ref, top_ref
):
    step = pl.program_id(0)
    gram = jnp.concatenate([gram_ref[0], gram_ref[1]], axis=1)
    taken = product(halves(weights_ref[...]), gram)
    trailing_ref[...] = by_turn(current_ref[...] - taken, owners)

    @pl.when(step == 0)
    def _():
        top_ref[...] = jnp.zeros_like(top_ref)

    @pl.when(step == place_ref[0])
    def _():
        top = dot(inverse_ref[...], gram, ((1,), (0,)))
        row = lax.broadcasted_iota(jnp.int32, top.shape, 0)
        column = lax.broadcasted_iota(jnp.int32, top.shape, 1) + step * top.shape[1]
        top_ref[...] = jnp.where(column >= row // PANEL * PANEL, top, 0.0) * scale


def rest_kernel(
    scale, owners, before, place_ref, current_ref, weights_ref, inverse_ref, gram_ref, lead_ref,
    trailing_in, trailing_ref, top_ref, split_ref, out_ref, sems
):
    step, steps = pl.program_id(0), pl.num_programs(0)
    part = gram_ref.shape[2]
    slot = lax.rem(step, 2)

    def send(step, slot):
        columns = pl.ds(pl.multiple_of(before + step * part, LANES), part)
        return pltpu.make_async_copy(out_ref.at[slot], trailing_ref.at[:, columns], sems.at[slot])

    @pl.when(step == 0)
    def _():
        split_ref[0], split_ref[1] = halves(weights_ref[...])
        top_ref[...] = lead_ref[...]

    @pl.when(step >= 2)
    def _():
        send(step - 2, slot).wait()

    columns = pl.ds(pl.multiple_of(before + step * part, LANES), part)
    taken = product((split_ref[0], split_ref[1]), gram_ref[0])
    out_ref[slot] = by_turn(current_ref[:, columns] - taken, owners)
    send(step, slot).start()
    for s in range(part // LANES):
        tile = before // LANES + step * (part // LANES) + s

        @pl.when(tile // 2 == place_ref[0])
        def _():
            at = pl.ds(pl.multiple_of(lax.rem(tile, 2) * LANES, LANES), LANES)
            gram = gram_ref[0, :, s * LANES : (s + 1) * LANES]
            top_ref[:, at] = dot(inverse_ref[...], gram, ((1,), (0,))) * scale

    @pl.when(step == steps - 1)
    def _():
        send(step - 1, 1 - slot).wait()
        send(step, slot).wait()


def eliminate(scale, me_blk, owners, current, weights, inverse, corner, rest):
    rows, width = current.shape
    wide = width // owners
    groups, n, lanes = corner.shape
    part = rest.shape[2]
    before = groups * lanes

    def whole(*shape):
        return pl.BlockSpec(shape, lambda s, p: (0,) * len(shape))

    out_shape = [
        jax.ShapeDtypeStruct((rows, width), jnp.float32),
        jax.ShapeDtypeStruct((n, wide), jnp.float32),
    ]
    held = pl.BlockSpec(memory_space=pltpu.VMEM)
    columns = pl.BlockSpec((rows, wide), lambda s, p: (0, s))
    trailing, top = pl.pallas_call(
        functools.partial(lead_kernel, scale, owners),
        grid_spec=pltpu.PrefetchScalarGridSpec(
            num_scalar_prefetch=1,
            grid=(before // wide,),
            in_specs=[
                columns,
                held,
                held,
                pl.BlockSpec((wide // lanes, n, lanes), lambda s, p: (s, 0, 0)),
            ],
            out_specs=[columns, whole(n, wide)],
        ),
        out_shape=out_shape,
        compiler_params=pltpu.CompilerParams(vmem_limit_bytes=20 * 2**20),
        cost_estimate=pl.CostEstimate(
            flops=6 * rows * n * before, bytes_accessed=8 * 2**20, transcendentals=0
        ),
    )(me_blk.reshape(1), current, weights, inverse, corner)
    return pl.pallas_call(
        functools.partial(rest_kernel, scale, owners, before),
        grid_spec=pltpu.PrefetchScalarGridSpec(
            num_scalar_prefetch=1,
            grid=(groups,),
            in_specs=[
                held,
                held,
                held,
                pl.BlockSpec((1, n, part), lambda s, p: (s, 0, 0)),
                held,
                pl.BlockSpec(memory_space=pl.ANY),
            ],
            out_specs=[pl.BlockSpec(memory_space=pl.ANY), whole(n, wide)],
            scratch_shapes=[
                pltpu.VMEM((2, rows, n), jnp.bfloat16),
                pltpu.VMEM((2, rows, part), jnp.float32),
                pltpu.SemaphoreType.DMA((2,)),
            ],
        ),
        out_shape=out_shape,
        input_output_aliases={6: 0},
        compiler_params=pltpu.CompilerParams(vmem_limit_bytes=44 * 2**20),
        cost_estimate=pl.CostEstimate(
            flops=6 * rows * n * (width - before), bytes_accessed=16 * 2**20, transcendentals=0
        ),
    )(me_blk.reshape(1), current, weights, inverse, rest, top, trailing)


def body(matrix, signs, tile_rows, tile_owner):
    rows_dev, width = matrix.shape
    groups = lax.axis_size("grp")
    owners = lax.axis_size("blk")
    me = lax.axis_index("grp")
    me_blk = lax.axis_index("blk")
    zed, core = me // 2, me % 2
    quads = groups // 2
    tiles = tile_owner.shape[1]
    per_source = TILE // owners
    picked = tiles * per_source
    part = width // groups

    wanted = tile_rows[0].reshape(tiles, per_source, owners)
    selector = jnp.arange(owners, dtype=jnp.int32) == me_blk
    wanted = jnp.sum(jnp.where(selector, wanted, 0), axis=2).reshape(1, picked)
    wanted = jnp.broadcast_to(wanted.astype(jnp.float32), (8, picked))
    pieces = split_columns(zed, matrix, signs, wanted, quads, 0, LANES)
    first = exchange(pieces, core)
    pieces = split_columns(zed, matrix, signs, wanted, quads, groups * LANES, part - LANES)
    later = exchange(pieces, core)
    lead, select = sample_first(me, rows_dev, picked, *first)

    flat = lead.reshape(groups * picked, LANES)
    leads = []
    for d in range(quads):
        mine = swap(flat, "grp", 2 * d) if d else flat
        leads += [mine, swap(mine, "grp", 1)]
    sampled, *backs = sample(me, select, *later, lead)
    partial = gram_part(me, sampled.reshape(groups * picked, part), leads)

    share = WIDE // owners
    partial = partial.reshape(owners, share, part)
    partial, *backs = lax.optimization_barrier((partial, *backs))
    summands = lax.all_to_all(partial, "blk", 0, 0, tiled=True)
    backs = [swap(backs[d], "grp", 2 * d) if d else backs[d] for d in range(quads)]
    give = jnp.stack([lax.dynamic_index_in_dim(x, 1 - core, 0, keepdims=False) for x in backs])
    give = swap(give, "grp", 1)
    owner_list = tile_owner[0]
    same = owner_list[:, None] == owner_list[None, :]
    order = jnp.arange(tiles, dtype=jnp.int32)
    rank = jnp.sum((same & (order[None, :] < order[:, None])).astype(jnp.int32), axis=1)
    place = owner_list * MAXT + rank
    hit = place[None, :] == jnp.arange(owners * MAXT, dtype=jnp.int32)[:, None]
    tile_of = jnp.max(jnp.where(hit, order[None, :], -1), axis=1)
    outgoing = pack(me, tile_of, backs, give, per_source)
    outgoing = outgoing.reshape(owners, MAXT * per_source, width)
    outgoing, summands = lax.optimization_barrier((outgoing, summands))
    gram = jnp.sum(summands, axis=0)
    rest = lax.all_gather(gram[:, LANES:], ("grp", "blk"), tiled=True)
    rest = rest.reshape(groups, WIDE, part - LANES)
    corner = gram[:, :LANES][None]
    for axis, strides in (("blk", (1, 2, 3)), ("blk", (4, 8, 12)), ("grp", (2, 4, 6))):
        corner = jnp.stack([corner] + [swap(corner, axis, d) for d in strides])
        corner = corner.reshape(-1, share, LANES)
        if strides == (4, 8, 12):
            corner, outgoing = lax.optimization_barrier((corner, outgoing))
    corner = corner.reshape(quads, owners, share, LANES)
    inverse, corner = inverse_of_factor(jnp.stack([me, me_blk]), corner, swap(corner, "grp", 1))

    current = lax.all_to_all(outgoing, "blk", 0, 0, tiled=True)
    current = current.reshape(MAXT * TILE, width)

    basis = dot(current[:, :WIDE], inverse, ((1,), (1,)))
    weights = dot(basis, inverse, ((1,), (0,)))
    scale = 1.0 / math.sqrt(groups * owners * TILE)
    trailing, top = eliminate(scale, me_blk, owners, current, weights, inverse, corner, rest)
    return (top, trailing)


def solution(mesh):
    in_specs = (P(("grp", "blk"), None), P(("grp", "blk")), P("grp", None, None), P("grp", None))
    out_specs = (P(None, "blk"), P(("grp", "blk"), None))
    return jax.shard_map(body, mesh=mesh, in_specs=in_specs, out_specs=out_specs, check_vma=False)
```

```python
import functools
import math

import jax
import jax.numpy as jnp
from jax import lax
from jax.experimental import pallas as pl
from jax.experimental.pallas import tpu as pltpu
from jax.sharding import PartitionSpec as P

TILE = 128
MAXT = 2
PANEL = 128
NPAN = 6
WIDE = PANEL * NPAN
LANES = 128
HI = lax.Precision.HIGHEST


def dot(a, b, dims, precision=HI):
    return lax.dot_general(
        a, b, (dims, ((), ())), precision=precision, preferred_element_type=jnp.float32
    )


def inverse_factor(block):
    n, some = block.shape[0], 16
    sub = lax.broadcasted_iota(jnp.int32, (n, n), 0)
    lane = lax.broadcasted_iota(jnp.int32, (n, n), 1)
    row = lax.broadcasted_iota(jnp.int32, (some, n), 0)
    left, right = block, (sub == lane).astype(jnp.float32)
    rows = []
    for base in range(0, n, some):
        top_left, top_right = left[:some], right[:some]
        cols = [
            jnp.broadcast_to(top_left[:, base + k : base + k + 1], (some, n)) for k in range(some)
        ]
        pivots = jnp.zeros((some, n), jnp.float32)
        for j in range(some):
            pivot = cols[j][j : j + 1]
            pivots = jnp.where(row == j, pivot, pivots)
            if j == some - 1:
                break
            factor = jnp.where(row > j, cols[j] * (1.0 / pivot), 0.0)
            for k in range(j + 1, some):
                cols[k] = cols[k] - factor * cols[k][j : j + 1]
            top_left = top_left - factor * top_left[j : j + 1]
            top_right = top_right - factor * top_right[j : j + 1]
        scale = lax.rsqrt(pivots)
        top_left, top_right = top_left * scale, top_right * scale
        rows.append(top_right)
        if base + some < n:
            turned = top_left.T
            left, right = left[some:], right[some:]
            for k in range(some):
                col = turned[base + some :, k : k + 1]
                left = left - col * top_left[k : k + 1]
                right = right - col * top_right[k : k + 1]
    return jnp.concatenate(rows, axis=0)


def factor_kernel(place_ref, own_ref, other_ref, inv_ref, corner_ref, work_ref):
    me, me_blk = place_ref[0], place_ref[1]
    quads, owners, share, lanes = own_ref.shape
    n = owners * share
    for tile in range(2 * quads):
        far = me ^ tile
        for owner in range(owners):
            rows = slice(owner * share, (owner + 1) * share)
            near = me_blk ^ owner
            piece = jnp.where(far % 2 == 0, own_ref[far // 2, near], other_ref[far // 2, near])
            corner_ref[tile, rows, :] = piece
            if tile * lanes < n:
                work_ref[rows, tile * lanes : (tile + 1) * lanes] = piece
    inv_ref[...] = jnp.zeros_like(inv_ref)
    for low in range(0, n, PANEL):
        high = low + PANEL
        inverse = inverse_factor(work_ref[low:high, low:high])
        inv_ref[low:high, low:high] = inverse
        if low:
            inv_ref[low:high, :low] = dot(inverse, inv_ref[low:high, :low], ((1,), (0,)))
        if high < n:
            upper = dot(inverse, work_ref[low:high, high:], ((1,), (0,)))
            work_ref[high:, high:] -= dot(upper, upper, ((0,), (0,)))
            inv_ref[high:, :high] -= dot(upper, inv_ref[low:high, :high], ((0,), (0,)))


def inverse_of_factor(place, own, other):
    quads, owners, share, lanes = own.shape
    n = owners * share
    return pl.pallas_call(
        factor_kernel,
        out_shape=(
            jax.ShapeDtypeStruct((n, n), jnp.float32),
            jax.ShapeDtypeStruct((2 * quads, n, lanes), jnp.float32),
        ),
        in_specs=[pl.BlockSpec(memory_space=pltpu.SMEM)]
        + [pl.BlockSpec(memory_space=pltpu.VMEM)] * 2,
        out_specs=(pl.BlockSpec(memory_space=pltpu.VMEM), pl.BlockSpec(memory_space=pltpu.VMEM)),
        scratch_shapes=[pltpu.VMEM((n, n), jnp.float32)],
        compiler_params=pltpu.CompilerParams(vmem_limit_bytes=32 * 2**20),
        cost_estimate=pl.CostEstimate(
            flops=10**9, bytes_accessed=6 * 2**20, transcendentals=0
        ),
    )(place, own, other)


def swap(x, axis, d):
    return lax.ppermute(x, axis, [(i, i ^ d) for i in range(lax.axis_size(axis))])


def exchange(pieces, core):
    kept = [swap(x, "grp", 2 * d) if d else x for d, x in enumerate(pieces)]
    other = [lax.dynamic_index_in_dim(x, 1 - core, 0, keepdims=False) for x in kept]
    return kept, [swap(x, "grp", 1) for x in other]


def parity(x):
    for shift in (4, 2, 1):
        x = x ^ lax.shift_right_logical(x, shift)
    return x & 1


def split_kernel(quads, per, place_ref, sign_ref, extra_ref, *refs):
    sources, outs = refs[: quads * per], refs[quads * per :]
    rows = sign_ref.shape[0]
    sign = sign_ref[...].astype(jnp.float32)
    for d, out in enumerate(outs):
        half = out.shape[2]
        for s, source in enumerate(sources[d * per : (d + 1) * per]):
            signed = source[...] * sign
            for part in range(2):
                core, at = divmod((2 * s + part) * LANES, half)
                out[core, :rows, at : at + LANES] = signed[:, part * LANES : (part + 1) * LANES]
        if out.shape[1] > rows:
            out[0, rows:, :] = extra_ref[...]
            out[1, rows:, :] = extra_ref[...]


def split_columns(zed, matrix, signs, extra, quads, first, part):
    rows = matrix.shape[0]
    block = 2 * LANES
    per = 2 * part // block
    reads = [
        pl.BlockSpec(
            (rows, block), lambda i, z, d=d, s=s: (0, first // block + (z[0] ^ d) * per + s)
        )
        for d in range(quads)
        for s in range(per)
    ]
    shape = (2, rows + (8 if extra.shape[1] == part else 0), part)
    return pl.pallas_call(
        functools.partial(split_kernel, quads, per),
        grid_spec=pltpu.PrefetchScalarGridSpec(
            num_scalar_prefetch=1,
            grid=(1,),
            in_specs=[pl.BlockSpec((rows, 1), lambda i, z: (0, 0))]
            + [pl.BlockSpec(extra.shape, lambda i, z: (0, 0))]
            + reads,
            out_specs=[pl.BlockSpec(shape, lambda i, z: (0, 0, 0))] * quads,
        ),
        out_shape=[jax.ShapeDtypeStruct(shape, jnp.float32)] * quads,
        compiler_params=pltpu.CompilerParams(vmem_limit_bytes=32 * 2**20),
        cost_estimate=pl.CostEstimate(
            flops=2 * quads * rows * part,
            bytes_accessed=16 * quads * rows * part,
            transcendentals=0,
        ),
    )(zed.reshape(1), signs.reshape(rows, 1), extra, *[matrix] * (quads * per))


def sample_first_kernel(scale, quads, place_ref, *refs):
    kept, given = refs[:quads], refs[quads : 2 * quads]
    sampled_ref, select_ref, mixed_ref = refs[2 * quads :]
    groups, picked, rows = select_ref.shape
    me = place_ref[0]
    column = lax.broadcasted_iota(jnp.int32, (picked, rows), 1)
    for d in range(quads):
        for e in range(2):
            lists = given[d][rows:, :] if e else kept[d][0, rows:, :]
            wanted = lists.T[:, :1].astype(jnp.int32)
            group = me ^ (2 * d + e)
            odd = parity(jnp.maximum(wanted, 0) & column) ^ parity(group & me)
            select = jnp.where(wanted >= 0, 1 - 2 * odd, 0)
            select_ref[group] = select.astype(jnp.float32).astype(jnp.bfloat16)
    sample_kernel(scale, quads, False, place_ref, select_ref, *kept, *given, sampled_ref, mixed_ref)


def sample_first(me, rows, picked, kept, given):
    quads = len(kept)
    groups = 2 * quads
    sent, block = given[0].shape

    def whole(*shape):
        return pl.BlockSpec(shape, lambda s, p: (0,) * len(shape))

    shapes = [(groups, picked, block), (groups, picked, rows)]
    return pl.pallas_call(
        functools.partial(sample_first_kernel, 1.0 / math.sqrt(groups * rows), quads),
        grid_spec=pltpu.PrefetchScalarGridSpec(
            num_scalar_prefetch=1,
            grid=(1,),
            in_specs=[pl.BlockSpec((1, sent, block), lambda s, p: (p[0] % 2, 0, 0))] * quads
            + [whole(sent, block)] * quads,
            out_specs=[whole(*shape) for shape in shapes],
            scratch_shapes=[pltpu.VMEM((groups, rows, block), jnp.float32)],
        ),
        out_shape=[
            jax.ShapeDtypeStruct(shapes[0], jnp.float32),
            jax.ShapeDtypeStruct(shapes[1], jnp.bfloat16),
        ],
        compiler_params=pltpu.CompilerParams(vmem_limit_bytes=24 * 2**20),
        cost_estimate=pl.CostEstimate(
            flops=6 * groups * picked * rows * block, bytes_accessed=4 * 2**20, transcendentals=0
        ),
    )(me.reshape(1), *kept, *given)


def sample_kernel(scale, quads, has_early, place_ref, select_ref, *refs):
    mixed_ref = refs[-1]
    groups, rows, width = mixed_ref.shape
    kept, given = refs[:quads], refs[quads : 2 * quads]
    early_ref = refs[2 * quads] if has_early else None
    sampled_ref = refs[2 * quads + has_early]
    backs = refs[2 * quads + has_early + 1 : -1]
    step = 16 if width <= 128 else 8

    def mix(r, carry):
        at = pl.ds(pl.multiple_of(r * step, step), step)
        parts = []
        for d in range(quads):
            parts += [kept[d][0, at, :], given[d][at, :]]
        level = 1
        while level < groups:
            new = list(parts)
            for k in range(groups):
                if not k & level:
                    new[k] = parts[k] + parts[k | level]
                    new[k | level] = parts[k] - parts[k | level]
            parts = new
            level *= 2
        for k in range(groups):
            mixed_ref[k, at, :] = parts[k]
        return carry

    lax.fori_loop(0, rows // step, mix, 0)
    zed = place_ref[0] // 2
    for d in range(quads):
        for c in range(2):
            group = 2 * (zed ^ d) + c
            left = select_ref[group]
            value = mixed_ref[group]
            total = None
            for _ in range(3):
                high = value.astype(jnp.bfloat16)
                term = jnp.dot(left, high, preferred_element_type=jnp.float32)
                total = term if total is None else total + term
                value = value - high.astype(jnp.float32)
            total = total * scale
            if early_ref is None:
                sampled_ref[group] = total
                continue
            early = early_ref[group]
            done = early.shape[1]
            sampled_ref[group, :, :done] = early
            sampled_ref[group, :, done:] = total
            backs[d][c, :, :done] = early
            backs[d][c, :, done:] = total


def sample(me, select, kept, given, early):
    groups, picked, rows = select.shape
    quads = groups // 2
    block = given[0].shape[1]

    def whole(*shape):
        return pl.BlockSpec(shape, lambda s, p: (0,) * len(shape))

    in_specs = [whole(groups, picked, rows)]
    in_specs += [pl.BlockSpec((1, rows, block), lambda s, p: (p[0] % 2, 0, 0))] * quads
    in_specs += [whole(rows, block)] * quads
    in_specs.append(whole(*early.shape))
    part = block + early.shape[2]
    shapes = [(groups, picked, part)] + [(2, picked, part)] * quads
    return pl.pallas_call(
        functools.partial(sample_kernel, 1.0 / math.sqrt(groups * rows), quads, True),
        grid_spec=pltpu.PrefetchScalarGridSpec(
            num_scalar_prefetch=1,
            grid=(1,),
            in_specs=in_specs,
            out_specs=[whole(*shape) for shape in shapes],
            scratch_shapes=[pltpu.VMEM((groups, rows, block), jnp.float32)],
        ),
        out_shape=[jax.ShapeDtypeStruct(shape, jnp.float32) for shape in shapes],
        compiler_params=pltpu.CompilerParams(vmem_limit_bytes=40 * 2**20),
        cost_estimate=pl.CostEstimate(
            flops=6 * groups * picked * rows * block, bytes_accessed=9 * 2**20, transcendentals=0
        ),
    )(me.reshape(1), select, *kept, *given, early)


def gram_kernel(place_ref, rest_ref, *refs):
    leads, out_ref, all_ref = refs[:-2], refs[-2], refs[-1]
    for k, lead in enumerate(leads):
        tile = place_ref[0] ^ k

        @pl.when(tile < NPAN)
        def _():
            at = pl.ds(pl.multiple_of(tile * LANES, LANES), LANES)
            all_ref[:, at] = lead[...]

    out_ref[...] = dot(all_ref[...], rest_ref[...], ((0,), (0,)))


def gram_part(me, rest, leads):
    rows, part = rest.shape
    return pl.pallas_call(
        gram_kernel,
        out_shape=jax.ShapeDtypeStruct((WIDE, part), jnp.float32),
        in_specs=[pl.BlockSpec(memory_space=pltpu.SMEM)]
        + [pl.BlockSpec(memory_space=pltpu.VMEM)] * (1 + len(leads)),
        out_specs=pl.BlockSpec(memory_space=pltpu.VMEM),
        scratch_shapes=[pltpu.VMEM((rows, WIDE), jnp.float32)],
        compiler_params=pltpu.CompilerParams(vmem_limit_bytes=36 * 2**20),
        cost_estimate=pl.CostEstimate(
            flops=12 * rows * WIDE * part, bytes_accessed=8 * 2**20, transcendentals=0
        ),
    )(me.reshape(1), rest, *leads)


def pack_kernel(place_ref, tile_ref, *refs):
    out_ref, given_ref = refs[-1], refs[-2]
    kept = refs[:-2]
    quads = len(kept)
    places, per, width = out_ref.shape
    groups = 2 * quads
    rest = width // groups - LANES
    me = place_ref[0]

    def fill(q, carry):
        tile = tile_ref[q]
        at = pl.ds(pl.multiple_of(jnp.maximum(tile, 0) * per, per), per)
        for d in range(quads):
            for e in range(2):
                rows = given_ref[d, at, :] if e else kept[d][0, at, :]
                rows = jnp.where(tile >= 0, rows, 0.0)
                far = me ^ (2 * d + e)
                where = pl.ds(pl.multiple_of(far * LANES, LANES), LANES)
                out_ref[q, :, where] = rows[:, :LANES]
                column = groups * LANES + far * rest
                where = pl.ds(pl.multiple_of(column, LANES), rest)
                out_ref[q, :, where] = rows[:, LANES:]
        return carry

    lax.fori_loop(0, places, fill, 0)


def pack(me, tile_of, kept, given, per):
    places = tile_of.shape[0]
    quads, picked, part = given.shape
    width = 2 * quads * part
    whole = (quads, picked, part)
    return pl.pallas_call(
        pack_kernel,
        grid_spec=pltpu.PrefetchScalarGridSpec(
            num_scalar_prefetch=2,
            grid=(1,),
            in_specs=[pl.BlockSpec((1, picked, part), lambda s, p, t: (p[0] % 2, 0, 0))] * quads
            + [pl.BlockSpec(whole, lambda s, p, t: (0, 0, 0))],
            out_specs=pl.BlockSpec((places, per, width), lambda s, p, t: (0, 0, 0)),
        ),
        out_shape=jax.ShapeDtypeStruct((places, per, width), jnp.float32),
        compiler_params=pltpu.CompilerParams(vmem_limit_bytes=32 * 2**20),
        cost_estimate=pl.CostEstimate(flops=0, bytes_accessed=8 * 2**20, transcendentals=0),
    )(me.reshape(1), tile_of, *kept, given)


def halves(x):
    high = x.astype(jnp.bfloat16)
    return high, (x - high.astype(jnp.float32)).astype(jnp.bfloat16)


def product(weights, gram):
    high, low = halves(gram)

    def term(a, b):
        return jnp.dot(a, b, preferred_element_type=jnp.float32)

    return term(weights[0], high) + (term(weights[0], low) + term(weights[1], high))


def by_turn(value, owners):
    rows, columns = value.shape
    value = value.reshape(owners, rows // owners, columns)
    return jnp.swapaxes(value, 0, 1).reshape(rows, columns)


def lead_kernel(
    scale, owners, place_ref, current_ref, weights_ref, inverse_ref, gram_ref, trailing_ref, top_ref
):
    step = pl.program_id(0)
    gram = jnp.concatenate([gram_ref[0], gram_ref[1]], axis=1)
    taken = product(halves(weights_ref[...]), gram)
    trailing_ref[...] = by_turn(current_ref[...] - taken, owners)

    @pl.when(step == 0)
    def _():
        top_ref[...] = jnp.zeros_like(top_ref)

    @pl.when(step == place_ref[0])
    def _():
        top = dot(inverse_ref[...], gram, ((1,), (0,)))
        row = lax.broadcasted_iota(jnp.int32, top.shape, 0)
        column = lax.broadcasted_iota(jnp.int32, top.shape, 1) + step * top.shape[1]
        top_ref[...] = jnp.where(column >= row // PANEL * PANEL, top, 0.0) * scale


def rest_kernel(
    scale, owners, before, place_ref, weights_ref, lead_ref, current_any, inverse_any, gram_any, _,
    trailing_ref, top_ref, split_ref, current_ref, inverse_ref, gram_ref, out_ref, sems, sent
):
    step = pl.program_id(0)
    steps, n, part = gram_ref.shape
    slot = lax.rem(step, 2)

    def columns(step):
        return pl.ds(pl.multiple_of(before + step * part, LANES), part)

    def fetch(step):
        return (
            pltpu.make_async_copy(gram_any.at[step], gram_ref.at[step], sems.at[0, step]),
            pltpu.make_async_copy(
                current_any.at[:, columns(step)], current_ref.at[step], sems.at[1, step]
            ),
        )

    inverse = pltpu.make_async_copy(inverse_any, inverse_ref, sems.at[0, steps])

    def send(step, slot):
        return pltpu.make_async_copy(
            out_ref.at[slot], trailing_ref.at[:, columns(step)], sent.at[slot]
        )

    @pl.when(step == 0)
    def _():
        for k in range(steps):
            for copy in fetch(k):
                copy.start()
        inverse.start()
        split_ref[0], split_ref[1] = halves(weights_ref[...])
        top_ref[...] = lead_ref[...]

    for copy in fetch(step):
        copy.wait()

    @pl.when(step >= 2)
    def _():
        send(step - 2, slot).wait()

    taken = product((split_ref[0], split_ref[1]), gram_ref[step])
    out_ref[slot] = by_turn(current_ref[step] - taken, owners)
    send(step, slot).start()

    @pl.when(step == steps - 1)
    def _():
        inverse.wait()
        wide = top_ref.shape[1]
        tile = (place_ref[0] * wide - before) // LANES

        @pl.when(tile >= 0)
        def _():
            gram = []
            for s in range(wide // LANES):
                block, at = (tile + s) // (part // LANES), lax.rem(tile + s, part // LANES)
                gram.append(gram_ref[block, :, pl.ds(pl.multiple_of(at * LANES, LANES), LANES)])
            gram = jnp.concatenate(gram, axis=1)
            half = n // 2
            top_ref[:half] = scale * dot(inverse_ref[:half, :half], gram[:half], ((1,), (0,)))
            top_ref[half:] = scale * dot(inverse_ref[half:], gram, ((1,), (0,)))

        send(step - 1, 1 - slot).wait()
        send(step, slot).wait()


def eliminate(scale, me_blk, owners, current, weights, inverse, corner, rest):
    rows, width = current.shape
    wide = width // owners
    groups, n, lanes = corner.shape
    part = rest.shape[2]
    before = groups * lanes

    def whole(*shape):
        return pl.BlockSpec(shape, lambda s, p: (0,) * len(shape))

    out_shape = [
        jax.ShapeDtypeStruct((rows, width), jnp.float32),
        jax.ShapeDtypeStruct((n, wide), jnp.float32),
    ]
    held = pl.BlockSpec(memory_space=pltpu.VMEM)
    columns = pl.BlockSpec((rows, wide), lambda s, p: (0, s))
    trailing, top = pl.pallas_call(
        functools.partial(lead_kernel, scale, owners),
        grid_spec=pltpu.PrefetchScalarGridSpec(
            num_scalar_prefetch=1,
            grid=(before // wide,),
            in_specs=[
                columns,
                held,
                held,
                pl.BlockSpec((wide // lanes, n, lanes), lambda s, p: (s, 0, 0)),
            ],
            out_specs=[columns, whole(n, wide)],
        ),
        out_shape=out_shape,
        compiler_params=pltpu.CompilerParams(vmem_limit_bytes=20 * 2**20),
        cost_estimate=pl.CostEstimate(
            flops=6 * rows * n * before, bytes_accessed=8 * 2**20, transcendentals=0
        ),
    )(me_blk.reshape(1), current, weights, inverse, corner)
    some = pl.BlockSpec(memory_space=pl.ANY)
    return pl.pallas_call(
        functools.partial(rest_kernel, scale, owners, before),
        grid_spec=pltpu.PrefetchScalarGridSpec(
            num_scalar_prefetch=1,
            grid=(groups,),
            in_specs=[whole(rows, n), whole(n, wide)] + [some] * 4,
            out_specs=[some, whole(n, wide)],
            scratch_shapes=[
                pltpu.VMEM((2, rows, n), jnp.bfloat16),
                pltpu.VMEM((groups, rows, part), jnp.float32),
                pltpu.VMEM((n, n), jnp.float32),
                pltpu.VMEM((groups, n, part), jnp.float32),
                pltpu.VMEM((2, rows, part), jnp.float32),
                pltpu.SemaphoreType.DMA((2, groups + 1)),
                pltpu.SemaphoreType.DMA((2,)),
            ],
        ),
        out_shape=out_shape,
        input_output_aliases={6: 0},
        compiler_params=pltpu.CompilerParams(vmem_limit_bytes=44 * 2**20),
        cost_estimate=pl.CostEstimate(
            flops=6 * rows * n * (width - before), bytes_accessed=16 * 2**20, transcendentals=0
        ),
    )(me_blk.reshape(1), weights, top, current, inverse, rest, trailing)


def body(matrix, signs, tile_rows, tile_owner):
    rows_dev, width = matrix.shape
    groups = lax.axis_size("grp")
    owners = lax.axis_size("blk")
    me = lax.axis_index("grp")
    me_blk = lax.axis_index("blk")
    zed, core = me // 2, me % 2
    quads = groups // 2
    tiles = tile_owner.shape[1]
    per_source = TILE // owners
    picked = tiles * per_source
    part = width // groups

    wanted = tile_rows[0].reshape(tiles, per_source, owners)
    selector = jnp.arange(owners, dtype=jnp.int32) == me_blk
    wanted = jnp.sum(jnp.where(selector, wanted, 0), axis=2).reshape(1, picked)
    wanted = jnp.broadcast_to(wanted.astype(jnp.float32), (8, picked))
    pieces = split_columns(zed, matrix, signs, wanted, quads, 0, LANES)
    first = exchange(pieces, core)
    pieces = split_columns(zed, matrix, signs, wanted, quads, groups * LANES, part - LANES)
    later = exchange(pieces, core)
    lead, select = sample_first(me, rows_dev, picked, *first)

    flat = lead.reshape(groups * picked, LANES)
    leads = []
    for d in range(quads):
        mine = swap(flat, "grp", 2 * d) if d else flat
        leads += [mine, swap(mine, "grp", 1)]
    sampled, *backs = sample(me, select, *later, lead)
    partial = gram_part(me, sampled.reshape(groups * picked, part), leads)

    share = WIDE // owners
    partial = partial.reshape(owners, share, part)
    partial, *backs = lax.optimization_barrier((partial, *backs))
    summands = lax.all_to_all(partial, "blk", 0, 0, tiled=True)
    backs = [swap(backs[d], "grp", 2 * d) if d else backs[d] for d in range(quads)]
    give = jnp.stack([lax.dynamic_index_in_dim(x, 1 - core, 0, keepdims=False) for x in backs])
    give = swap(give, "grp", 1)
    owner_list = tile_owner[0]
    same = owner_list[:, None] == owner_list[None, :]
    order = jnp.arange(tiles, dtype=jnp.int32)
    rank = jnp.sum((same & (order[None, :] < order[:, None])).astype(jnp.int32), axis=1)
    place = owner_list * MAXT + rank
    hit = place[None, :] == jnp.arange(owners * MAXT, dtype=jnp.int32)[:, None]
    tile_of = jnp.max(jnp.where(hit, order[None, :], -1), axis=1)
    outgoing = pack(me, tile_of, backs, give, per_source)
    outgoing = outgoing.reshape(owners, MAXT * per_source, width)
    outgoing, summands = lax.optimization_barrier((outgoing, summands))
    gram = jnp.sum(summands, axis=0)
    rest = lax.all_gather(gram[:, LANES:], ("grp", "blk"), tiled=True)
    rest = rest.reshape(groups, WIDE, part - LANES)
    corner = gram[:, :LANES][None]
    for axis, strides in (("blk", (1, 2, 3)), ("blk", (4, 8, 12)), ("grp", (2, 4, 6))):
        corner = jnp.stack([corner] + [swap(corner, axis, d) for d in strides])
        corner = corner.reshape(-1, share, LANES)
        if strides == (4, 8, 12):
            corner, outgoing = lax.optimization_barrier((corner, outgoing))
    corner = corner.reshape(quads, owners, share, LANES)
    inverse, corner = inverse_of_factor(jnp.stack([me, me_blk]), corner, swap(corner, "grp", 1))

    current = lax.all_to_all(outgoing, "blk", 0, 0, tiled=True)
    current = current.reshape(MAXT * TILE, width)

    basis = dot(current[:, :WIDE], inverse, ((1,), (1,)))
    weights = dot(basis, inverse, ((1,), (0,)))
    scale = 1.0 / math.sqrt(groups * owners * TILE)
    trailing, top = eliminate(scale, me_blk, owners, current, weights, inverse, corner, rest)
    return (top, trailing)


def solution(mesh):
    in_specs = (P(("grp", "blk"), None), P(("grp", "blk")), P("grp", None, None), P("grp", None))
    out_specs = (P(None, "blk"), P(("grp", "blk"), None))
    return jax.shard_map(body, mesh=mesh, in_specs=in_specs, out_specs=out_specs, check_vma=False)
```

```python
import functools
import math

import jax
import jax.numpy as jnp
from jax import lax
from jax.experimental import pallas as pl
from jax.experimental.pallas import tpu as pltpu
from jax.sharding import PartitionSpec as P

TILE = 128
MAXT = 2
PANEL = 128
NPAN = 6
WIDE = PANEL * NPAN
LANES = 128
HI = lax.Precision.HIGHEST


def dot(a, b, dims, precision=HI):
    return lax.dot_general(
        a, b, (dims, ((), ())), precision=precision, preferred_element_type=jnp.float32
    )


def inverse_factor(block):
    n, some = block.shape[0], 16
    sub = lax.broadcasted_iota(jnp.int32, (n, n), 0)
    lane = lax.broadcasted_iota(jnp.int32, (n, n), 1)
    row = lax.broadcasted_iota(jnp.int32, (some, n), 0)
    left, right = block, (sub == lane).astype(jnp.float32)
    rows = []
    for base in range(0, n, some):
        top_left, top_right = left[:some], right[:some]
        cols = [
            jnp.broadcast_to(top_left[:, base + k : base + k + 1], (some, n)) for k in range(some)
        ]
        pivots = jnp.zeros((some, n), jnp.float32)
        for j in range(some):
            pivot = cols[j][j : j + 1]
            pivots = jnp.where(row == j, pivot, pivots)
            if j == some - 1:
                break
            factor = jnp.where(row > j, cols[j] * (1.0 / pivot), 0.0)
            for k in range(j + 1, some):
                cols[k] = cols[k] - factor * cols[k][j : j + 1]
            top_left = top_left - factor * top_left[j : j + 1]
            top_right = top_right - factor * top_right[j : j + 1]
        scale = lax.rsqrt(pivots)
        top_left, top_right = top_left * scale, top_right * scale
        rows.append(top_right)
        if base + some < n:
            turned = top_left.T
            left, right = left[some:], right[some:]
            for k in range(some):
                col = turned[base + some :, k : k + 1]
                left = left - col * top_left[k : k + 1]
                right = right - col * top_right[k : k + 1]
    return jnp.concatenate(rows, axis=0)


def factor_kernel(place_ref, own_ref, other_ref, inv_ref, corner_ref, work_ref):
    me, me_blk = place_ref[0], place_ref[1]
    quads, owners, share, lanes = own_ref.shape
    n = owners * share
    for tile in range(2 * quads):
        far = me ^ tile
        for owner in range(owners):
            rows = slice(owner * share, (owner + 1) * share)
            near = me_blk ^ owner
            piece = jnp.where(far % 2 == 0, own_ref[far // 2, near], other_ref[far // 2, near])
            corner_ref[tile, rows, :] = piece
            if tile * lanes < n:
                work_ref[rows, tile * lanes : (tile + 1) * lanes] = piece
    inv_ref[...] = jnp.zeros_like(inv_ref)
    for low in range(0, n, PANEL):
        high = low + PANEL
        inverse = inverse_factor(work_ref[low:high, low:high])
        inv_ref[low:high, low:high] = inverse
        if low:
            inv_ref[low:high, :low] = dot(inverse, inv_ref[low:high, :low], ((1,), (0,)))
        if high < n:
            upper = dot(inverse, work_ref[low:high, high:], ((1,), (0,)))
            work_ref[high:, high:] -= dot(upper, upper, ((0,), (0,)))
            inv_ref[high:, :high] -= dot(upper, inv_ref[low:high, :high], ((0,), (0,)))


def inverse_of_factor(place, own, other):
    quads, owners, share, lanes = own.shape
    n = owners * share
    return pl.pallas_call(
        factor_kernel,
        out_shape=(
            jax.ShapeDtypeStruct((n, n), jnp.float32),
            jax.ShapeDtypeStruct((2 * quads, n, lanes), jnp.float32),
        ),
        in_specs=[pl.BlockSpec(memory_space=pltpu.SMEM)]
        + [pl.BlockSpec(memory_space=pltpu.VMEM)] * 2,
        out_specs=(pl.BlockSpec(memory_space=pltpu.VMEM), pl.BlockSpec(memory_space=pltpu.VMEM)),
        scratch_shapes=[pltpu.VMEM((n, n), jnp.float32)],
        compiler_params=pltpu.CompilerParams(vmem_limit_bytes=32 * 2**20),
        cost_estimate=pl.CostEstimate(
            flops=10**9, bytes_accessed=6 * 2**20, transcendentals=0
        ),
    )(place, own, other)


def swap(x, axis, d):
    return lax.ppermute(x, axis, [(i, i ^ d) for i in range(lax.axis_size(axis))])


def exchange(pieces, core):
    kept = [swap(x, "grp", 2 * d) if d else x for d, x in enumerate(pieces)]
    other = [lax.dynamic_index_in_dim(x, 1 - core, 0, keepdims=False) for x in kept]
    return kept, [swap(x, "grp", 1) for x in other]


def parity(x):
    for shift in (4, 2, 1):
        x = x ^ lax.shift_right_logical(x, shift)
    return x & 1


def split_kernel(quads, per, place_ref, sign_ref, extra_ref, *refs):
    sources, outs = refs[: quads * per], refs[quads * per :]
    rows = sign_ref.shape[0]
    sign = sign_ref[...].astype(jnp.float32)
    for d, out in enumerate(outs):
        half = out.shape[2]
        for s, source in enumerate(sources[d * per : (d + 1) * per]):
            signed = source[...] * sign
            for part in range(2):
                core, at = divmod((2 * s + part) * LANES, half)
                out[core, :rows, at : at + LANES] = signed[:, part * LANES : (part + 1) * LANES]
        if out.shape[1] > rows:
            out[0, rows:, :] = extra_ref[...]
            out[1, rows:, :] = extra_ref[...]


def split_columns(zed, matrix, signs, extra, quads, first, part):
    rows = matrix.shape[0]
    block = 2 * LANES
    per = 2 * part // block
    reads = [
        pl.BlockSpec(
            (rows, block), lambda i, z, d=d, s=s: (0, first // block + (z[0] ^ d) * per + s)
        )
        for d in range(quads)
        for s in range(per)
    ]
    shape = (2, rows + (8 if extra.shape[1] == part else 0), part)
    return pl.pallas_call(
        functools.partial(split_kernel, quads, per),
        grid_spec=pltpu.PrefetchScalarGridSpec(
            num_scalar_prefetch=1,
            grid=(1,),
            in_specs=[pl.BlockSpec((rows, 1), lambda i, z: (0, 0))]
            + [pl.BlockSpec(extra.shape, lambda i, z: (0, 0))]
            + reads,
            out_specs=[pl.BlockSpec(shape, lambda i, z: (0, 0, 0))] * quads,
        ),
        out_shape=[jax.ShapeDtypeStruct(shape, jnp.float32)] * quads,
        compiler_params=pltpu.CompilerParams(vmem_limit_bytes=32 * 2**20),
        cost_estimate=pl.CostEstimate(
            flops=2 * quads * rows * part,
            bytes_accessed=16 * quads * rows * part,
            transcendentals=0,
        ),
    )(zed.reshape(1), signs.reshape(rows, 1), extra, *[matrix] * (quads * per))


def sample_first_kernel(scale, quads, place_ref, *refs):
    kept, given = refs[:quads], refs[quads : 2 * quads]
    sampled_ref, select_ref, mixed_ref = refs[2 * quads :]
    groups, picked, rows = select_ref.shape
    me = place_ref[0]
    column = lax.broadcasted_iota(jnp.int32, (picked, rows), 1)
    for d in range(quads):
        for e in range(2):
            lists = given[d][rows:, :] if e else kept[d][0, rows:, :]
            wanted = lists.T[:, :1].astype(jnp.int32)
            group = me ^ (2 * d + e)
            odd = parity(jnp.maximum(wanted, 0) & column) ^ parity(group & me)
            select = jnp.where(wanted >= 0, 1 - 2 * odd, 0)
            select_ref[group] = select.astype(jnp.float32).astype(jnp.bfloat16)
    sample_kernel(scale, quads, False, place_ref, select_ref, *kept, *given, sampled_ref, mixed_ref)


def sample_first(me, rows, picked, kept, given):
    quads = len(kept)
    groups = 2 * quads
    sent, block = given[0].shape

    def whole(*shape):
        return pl.BlockSpec(shape, lambda s, p: (0,) * len(shape))

    shapes = [(groups, picked, block), (groups, picked, rows)]
    return pl.pallas_call(
        functools.partial(sample_first_kernel, 1.0 / math.sqrt(groups * rows), quads),
        grid_spec=pltpu.PrefetchScalarGridSpec(
            num_scalar_prefetch=1,
            grid=(1,),
            in_specs=[pl.BlockSpec((1, sent, block), lambda s, p: (p[0] % 2, 0, 0))] * quads
            + [whole(sent, block)] * quads,
            out_specs=[whole(*shape) for shape in shapes],
            scratch_shapes=[pltpu.VMEM((groups, rows, block), jnp.float32)],
        ),
        out_shape=[
            jax.ShapeDtypeStruct(shapes[0], jnp.float32),
            jax.ShapeDtypeStruct(shapes[1], jnp.bfloat16),
        ],
        compiler_params=pltpu.CompilerParams(vmem_limit_bytes=24 * 2**20),
        cost_estimate=pl.CostEstimate(
            flops=6 * groups * picked * rows * block, bytes_accessed=4 * 2**20, transcendentals=0
        ),
    )(me.reshape(1), *kept, *given)


def sample_kernel(scale, quads, has_early, place_ref, select_ref, *refs):
    mixed_ref = refs[-1]
    groups, rows, width = mixed_ref.shape
    kept, given = refs[:quads], refs[quads : 2 * quads]
    early_ref = refs[2 * quads] if has_early else None
    sampled_ref = refs[2 * quads + has_early]
    backs = refs[2 * quads + has_early + 1 : -1]
    step = 16 if width <= 128 else 8

    def mix(r, carry):
        at = pl.ds(pl.multiple_of(r * step, step), step)
        parts = []
        for d in range(quads):
            parts += [kept[d][0, at, :], given[d][at, :]]
        level = 1
        while level < groups:
            new = list(parts)
            for k in range(groups):
                if not k & level:
                    new[k] = parts[k] + parts[k | level]
                    new[k | level] = parts[k] - parts[k | level]
            parts = new
            level *= 2
        for k in range(groups):
            mixed_ref[k, at, :] = parts[k]
        return carry

    lax.fori_loop(0, rows // step, mix, 0)
    zed = place_ref[0] // 2
    for d in range(quads):
        for c in range(2):
            group = 2 * (zed ^ d) + c
            left = select_ref[group]
            value = mixed_ref[group]
            total = None
            for _ in range(3):
                high = value.astype(jnp.bfloat16)
                term = jnp.dot(left, high, preferred_element_type=jnp.float32)
                total = term if total is None else total + term
                value = value - high.astype(jnp.float32)
            total = total * scale
            if early_ref is None:
                sampled_ref[group] = total
                continue
            early = early_ref[group]
            done = early.shape[1]
            sampled_ref[group, :, :done] = early
            sampled_ref[group, :, done:] = total
            backs[d][c, :, :done] = early
            backs[d][c, :, done:] = total


def sample(me, select, kept, given, early):
    groups, picked, rows = select.shape
    quads = groups // 2
    block = given[0].shape[1]

    def whole(*shape):
        return pl.BlockSpec(shape, lambda s, p: (0,) * len(shape))

    in_specs = [whole(groups, picked, rows)]
    in_specs += [pl.BlockSpec((1, rows, block), lambda s, p: (p[0] % 2, 0, 0))] * quads
    in_specs += [whole(rows, block)] * quads
    in_specs.append(whole(*early.shape))
    part = block + early.shape[2]
    shapes = [(groups, picked, part)] + [(2, picked, part)] * quads
    return pl.pallas_call(
        functools.partial(sample_kernel, 1.0 / math.sqrt(groups * rows), quads, True),
        grid_spec=pltpu.PrefetchScalarGridSpec(
            num_scalar_prefetch=1,
            grid=(1,),
            in_specs=in_specs,
            out_specs=[whole(*shape) for shape in shapes],
            scratch_shapes=[pltpu.VMEM((groups, rows, block), jnp.float32)],
        ),
        out_shape=[jax.ShapeDtypeStruct(shape, jnp.float32) for shape in shapes],
        compiler_params=pltpu.CompilerParams(vmem_limit_bytes=40 * 2**20),
        cost_estimate=pl.CostEstimate(
            flops=6 * groups * picked * rows * block, bytes_accessed=9 * 2**20, transcendentals=0
        ),
    )(me.reshape(1), select, *kept, *given, early)


def gram_kernel(place_ref, rest_ref, *refs):
    leads, out_ref, all_ref = refs[:-2], refs[-2], refs[-1]
    for k, lead in enumerate(leads):
        tile = place_ref[0] ^ k

        @pl.when(tile < NPAN)
        def _():
            at = pl.ds(pl.multiple_of(tile * LANES, LANES), LANES)
            all_ref[:, at] = lead[...]

    out_ref[...] = dot(all_ref[...], rest_ref[...], ((0,), (0,)))


def gram_part(me, rest, leads):
    rows, part = rest.shape
    return pl.pallas_call(
        gram_kernel,
        out_shape=jax.ShapeDtypeStruct((WIDE, part), jnp.float32),
        in_specs=[pl.BlockSpec(memory_space=pltpu.SMEM)]
        + [pl.BlockSpec(memory_space=pltpu.VMEM)] * (1 + len(leads)),
        out_specs=pl.BlockSpec(memory_space=pltpu.VMEM),
        scratch_shapes=[pltpu.VMEM((rows, WIDE), jnp.float32)],
        compiler_params=pltpu.CompilerParams(vmem_limit_bytes=36 * 2**20),
        cost_estimate=pl.CostEstimate(
            flops=12 * rows * WIDE * part, bytes_accessed=8 * 2**20, transcendentals=0
        ),
    )(me.reshape(1), rest, *leads)


def pack_kernel(place_ref, tile_ref, *refs):
    out_ref, given_ref = refs[-1], refs[-2]
    kept = refs[:-2]
    quads = len(kept)
    places, per, width = out_ref.shape
    groups = 2 * quads
    rest = width // groups - LANES
    me = place_ref[0]

    def fill(q, carry):
        tile = tile_ref[q]
        at = pl.ds(pl.multiple_of(jnp.maximum(tile, 0) * per, per), per)
        for d in range(quads):
            for e in range(2):
                rows = given_ref[d, at, :] if e else kept[d][0, at, :]
                rows = jnp.where(tile >= 0, rows, 0.0)
                far = me ^ (2 * d + e)
                where = pl.ds(pl.multiple_of(far * LANES, LANES), LANES)
                out_ref[q, :, where] = rows[:, :LANES]
                column = groups * LANES + far * rest
                where = pl.ds(pl.multiple_of(column, LANES), rest)
                out_ref[q, :, where] = rows[:, LANES:]
        return carry

    lax.fori_loop(0, places, fill, 0)


def pack(me, tile_of, kept, given, per):
    places = tile_of.shape[0]
    quads, picked, part = given.shape
    width = 2 * quads * part
    whole = (quads, picked, part)
    return pl.pallas_call(
        pack_kernel,
        grid_spec=pltpu.PrefetchScalarGridSpec(
            num_scalar_prefetch=2,
            grid=(1,),
            in_specs=[pl.BlockSpec((1, picked, part), lambda s, p, t: (p[0] % 2, 0, 0))] * quads
            + [pl.BlockSpec(whole, lambda s, p, t: (0, 0, 0))],
            out_specs=pl.BlockSpec((places, per, width), lambda s, p, t: (0, 0, 0)),
        ),
        out_shape=jax.ShapeDtypeStruct((places, per, width), jnp.float32),
        compiler_params=pltpu.CompilerParams(vmem_limit_bytes=32 * 2**20),
        cost_estimate=pl.CostEstimate(flops=0, bytes_accessed=8 * 2**20, transcendentals=0),
    )(me.reshape(1), tile_of, *kept, given)


def halves(x):
    high = x.astype(jnp.bfloat16)
    return high, (x - high.astype(jnp.float32)).astype(jnp.bfloat16)


def product(weights, gram):
    high, low = halves(gram)

    def term(a, b):
        return jnp.dot(a, b, preferred_element_type=jnp.float32)

    return term(weights[0], high) + (term(weights[0], low) + term(weights[1], high))


def by_turn(value, owners):
    rows, columns = value.shape
    value = value.reshape(owners, rows // owners, columns)
    return jnp.swapaxes(value, 0, 1).reshape(rows, columns)


def lead_kernel(
    scale, owners, place_ref, current_ref, weights_ref, inverse_ref, gram_ref, trailing_ref, top_ref
):
    step = pl.program_id(0)
    gram = jnp.concatenate([gram_ref[0], gram_ref[1]], axis=1)
    taken = product(halves(weights_ref[...]), gram)
    trailing_ref[...] = by_turn(current_ref[...] - taken, owners)

    @pl.when(step == 0)
    def _():
        top_ref[...] = jnp.zeros_like(top_ref)

    @pl.when(step == place_ref[0])
    def _():
        top = dot(inverse_ref[...], gram, ((1,), (0,)))
        row = lax.broadcasted_iota(jnp.int32, top.shape, 0)
        column = lax.broadcasted_iota(jnp.int32, top.shape, 1) + step * top.shape[1]
        top_ref[...] = jnp.where(column >= row // PANEL * PANEL, top, 0.0) * scale


def rest_kernel(
    scale, owners, before, place_ref, weights_ref, lead_any, current_any, inverse_any, gram_any, _,
    trailing_ref, top_ref, split_ref, current_ref, inverse_ref, gram_ref, out_ref, sems, sent
):
    step = pl.program_id(0)
    steps, n, part = gram_ref.shape
    slot = lax.rem(step, 2)

    def columns(step):
        return pl.ds(pl.multiple_of(before + step * part, LANES), part)

    def fetch(step):
        return (
            pltpu.make_async_copy(gram_any.at[step], gram_ref.at[step], sems.at[0, step]),
            pltpu.make_async_copy(
                current_any.at[:, columns(step)], current_ref.at[step], sems.at[1, step]
            ),
        )

    inverse = pltpu.make_async_copy(inverse_any, inverse_ref, sems.at[0, steps])
    lead = pltpu.make_async_copy(lead_any, top_ref, sems.at[1, steps])

    def send(step, slot):
        return pltpu.make_async_copy(
            out_ref.at[slot], trailing_ref.at[:, columns(step)], sent.at[slot]
        )

    @pl.when(step == 0)
    def _():
        for k in range(steps):
            for copy in fetch(k):
                copy.start()
        inverse.start()
        lead.start()
        split_ref[0], split_ref[1] = halves(weights_ref[...])

    for copy in fetch(step):
        copy.wait()

    @pl.when(step >= 2)
    def _():
        send(step - 2, slot).wait()

    taken = product((split_ref[0], split_ref[1]), gram_ref[step])
    out_ref[slot] = by_turn(current_ref[step] - taken, owners)
    send(step, slot).start()

    @pl.when(step == steps - 1)
    def _():
        inverse.wait()
        lead.wait()
        wide = top_ref.shape[1]
        tile = (place_ref[0] * wide - before) // LANES

        @pl.when(tile >= 0)
        def _():
            gram = []
            for s in range(wide // LANES):
                block, at = (tile + s) // (part // LANES), lax.rem(tile + s, part // LANES)
                gram.append(gram_ref[block, :, pl.ds(pl.multiple_of(at * LANES, LANES), LANES)])
            gram = jnp.concatenate(gram, axis=1)
            half = n // 2
            top_ref[:half] = scale * dot(inverse_ref[:half, :half], gram[:half], ((1,), (0,)))
            top_ref[half:] = scale * dot(inverse_ref[half:], gram, ((1,), (0,)))

        send(step - 1, 1 - slot).wait()
        send(step, slot).wait()


def eliminate(scale, me_blk, owners, current, weights, inverse, corner, rest):
    rows, width = current.shape
    wide = width // owners
    groups, n, lanes = corner.shape
    part = rest.shape[2]
    before = groups * lanes

    def whole(*shape):
        return pl.BlockSpec(shape, lambda s, p: (0,) * len(shape))

    out_shape = [
        jax.ShapeDtypeStruct((rows, width), jnp.float32),
        jax.ShapeDtypeStruct((n, wide), jnp.float32),
    ]
    held = pl.BlockSpec(memory_space=pltpu.VMEM)
    columns = pl.BlockSpec((rows, wide), lambda s, p: (0, s))
    trailing, top = pl.pallas_call(
        functools.partial(lead_kernel, scale, owners),
        grid_spec=pltpu.PrefetchScalarGridSpec(
            num_scalar_prefetch=1,
            grid=(before // wide,),
            in_specs=[
                columns,
                held,
                held,
                pl.BlockSpec((wide // lanes, n, lanes), lambda s, p: (s, 0, 0)),
            ],
            out_specs=[columns, whole(n, wide)],
        ),
        out_shape=out_shape,
        compiler_params=pltpu.CompilerParams(vmem_limit_bytes=20 * 2**20),
        cost_estimate=pl.CostEstimate(
            flops=6 * rows * n * before, bytes_accessed=8 * 2**20, transcendentals=0
        ),
    )(me_blk.reshape(1), current, weights, inverse, corner)
    some = pl.BlockSpec(memory_space=pl.ANY)
    return pl.pallas_call(
        functools.partial(rest_kernel, scale, owners, before),
        grid_spec=pltpu.PrefetchScalarGridSpec(
            num_scalar_prefetch=1,
            grid=(groups,),
            in_specs=[whole(rows, n)] + [some] * 5,
            out_specs=[some, whole(n, wide)],
            scratch_shapes=[
                pltpu.VMEM((2, rows, n), jnp.bfloat16),
                pltpu.VMEM((groups, rows, part), jnp.float32),
                pltpu.VMEM((n, n), jnp.float32),
                pltpu.VMEM((groups, n, part), jnp.float32),
                pltpu.VMEM((2, rows, part), jnp.float32),
                pltpu.SemaphoreType.DMA((2, groups + 1)),
                pltpu.SemaphoreType.DMA((2,)),
            ],
        ),
        out_shape=out_shape,
        input_output_aliases={6: 0},
        compiler_params=pltpu.CompilerParams(vmem_limit_bytes=44 * 2**20),
        cost_estimate=pl.CostEstimate(
            flops=6 * rows * n * (width - before), bytes_accessed=16 * 2**20, transcendentals=0
        ),
    )(me_blk.reshape(1), weights, top, current, inverse, rest, trailing)


def body(matrix, signs, tile_rows, tile_owner):
    rows_dev, width = matrix.shape
    groups = lax.axis_size("grp")
    owners = lax.axis_size("blk")
    me = lax.axis_index("grp")
    me_blk = lax.axis_index("blk")
    zed, core = me // 2, me % 2
    quads = groups // 2
    tiles = tile_owner.shape[1]
    per_source = TILE // owners
    picked = tiles * per_source
    part = width // groups

    wanted = tile_rows[0].reshape(tiles, per_source, owners)
    selector = jnp.arange(owners, dtype=jnp.int32) == me_blk
    wanted = jnp.sum(jnp.where(selector, wanted, 0), axis=2).reshape(1, picked)
    wanted = jnp.broadcast_to(wanted.astype(jnp.float32), (8, picked))
    pieces = split_columns(zed, matrix, signs, wanted, quads, 0, LANES)
    first = exchange(pieces, core)
    pieces = split_columns(zed, matrix, signs, wanted, quads, groups * LANES, part - LANES)
    later = exchange(pieces, core)
    lead, select = sample_first(me, rows_dev, picked, *first)

    flat = lead.reshape(groups * picked, LANES)
    leads = []
    for d in range(quads):
        mine = swap(flat, "grp", 2 * d) if d else flat
        leads += [mine, swap(mine, "grp", 1)]
    sampled, *backs = sample(me, select, *later, lead)
    partial = gram_part(me, sampled.reshape(groups * picked, part), leads)

    share = WIDE // owners
    partial = partial.reshape(owners, share, part)
    partial, *backs = lax.optimization_barrier((partial, *backs))
    summands = lax.all_to_all(partial, "blk", 0, 0, tiled=True)
    backs = [swap(backs[d], "grp", 2 * d) if d else backs[d] for d in range(quads)]
    give = jnp.stack([lax.dynamic_index_in_dim(x, 1 - core, 0, keepdims=False) for x in backs])
    give = swap(give, "grp", 1)
    owner_list = tile_owner[0]
    same = owner_list[:, None] == owner_list[None, :]
    order = jnp.arange(tiles, dtype=jnp.int32)
    rank = jnp.sum((same & (order[None, :] < order[:, None])).astype(jnp.int32), axis=1)
    place = owner_list * MAXT + rank
    hit = place[None, :] == jnp.arange(owners * MAXT, dtype=jnp.int32)[:, None]
    tile_of = jnp.max(jnp.where(hit, order[None, :], -1), axis=1)
    outgoing = pack(me, tile_of, backs, give, per_source)
    outgoing = outgoing.reshape(owners, MAXT * per_source, width)
    outgoing, summands = lax.optimization_barrier((outgoing, summands))
    gram = jnp.sum(summands, axis=0)
    rest = lax.all_gather(gram[:, LANES:], ("grp", "blk"), tiled=True)
    rest = rest.reshape(groups, WIDE, part - LANES)
    corner = gram[:, :LANES][None]
    for axis, strides in (("blk", (1, 2, 3)), ("blk", (4, 8, 12)), ("grp", (2, 4, 6))):
        corner = jnp.stack([corner] + [swap(corner, axis, d) for d in strides])
        corner = corner.reshape(-1, share, LANES)
        if strides == (4, 8, 12):
            corner, outgoing = lax.optimization_barrier((corner, outgoing))
    corner = corner.reshape(quads, owners, share, LANES)
    inverse, corner = inverse_of_factor(jnp.stack([me, me_blk]), corner, swap(corner, "grp", 1))

    current = lax.all_to_all(outgoing, "blk", 0, 0, tiled=True)
    current = current.reshape(MAXT * TILE, width)

    basis = dot(current[:, :WIDE], inverse, ((1,), (1,)))
    weights = dot(basis, inverse, ((1,), (0,)))
    scale = 1.0 / math.sqrt(groups * owners * TILE)
    trailing, top = eliminate(scale, me_blk, owners, current, weights, inverse, corner, rest)
    return (top, trailing)


def solution(mesh):
    in_specs = (P(("grp", "blk"), None), P(("grp", "blk")), P("grp", None, None), P("grp", None))
    out_specs = (P(None, "blk"), P(("grp", "blk"), None))
    return jax.shard_map(body, mesh=mesh, in_specs=in_specs, out_specs=out_specs, check_vma=False)
```

```python
import functools
import math

import jax
import jax.numpy as jnp
from jax import lax
from jax.experimental import pallas as pl
from jax.experimental.pallas import tpu as pltpu
from jax.sharding import PartitionSpec as P

TILE = 128
MAXT = 2
PANEL = 128
NPAN = 6
WIDE = PANEL * NPAN
LANES = 128
HI = lax.Precision.HIGHEST


def dot(a, b, dims, precision=HI):
    return lax.dot_general(
        a, b, (dims, ((), ())), precision=precision, preferred_element_type=jnp.float32
    )


def inverse_factor(block):
    n, some = block.shape[0], 16
    sub = lax.broadcasted_iota(jnp.int32, (n, n), 0)
    lane = lax.broadcasted_iota(jnp.int32, (n, n), 1)
    row = lax.broadcasted_iota(jnp.int32, (some, n), 0)
    left, right = block, (sub == lane).astype(jnp.float32)
    rows = []
    for base in range(0, n, some):
        top_left, top_right = left[:some], right[:some]
        cols = [
            jnp.broadcast_to(top_left[:, base + k : base + k + 1], (some, n)) for k in range(some)
        ]
        pivots = jnp.zeros((some, n), jnp.float32)
        for j in range(some):
            pivot = cols[j][j : j + 1]
            pivots = jnp.where(row == j, pivot, pivots)
            if j == some - 1:
                break
            factor = jnp.where(row > j, cols[j] * (1.0 / pivot), 0.0)
            for k in range(j + 1, some):
                cols[k] = cols[k] - factor * cols[k][j : j + 1]
            top_left = top_left - factor * top_left[j : j + 1]
            top_right = top_right - factor * top_right[j : j + 1]
        scale = lax.rsqrt(pivots)
        top_left, top_right = top_left * scale, top_right * scale
        rows.append(top_right)
        if base + some < n:
            turned = top_left.T
            left, right = left[some:], right[some:]
            for k in range(some):
                col = turned[base + some :, k : k + 1]
                left = left - col * top_left[k : k + 1]
                right = right - col * top_right[k : k + 1]
    return jnp.concatenate(rows, axis=0)


def factor_kernel(place_ref, own_ref, other_ref, inv_ref, corner_ref, work_ref):
    me, me_blk = place_ref[0], place_ref[1]
    quads, owners, share, lanes = own_ref.shape
    n = owners * share
    for tile in range(2 * quads):
        far = me ^ tile
        for owner in range(owners):
            rows = slice(owner * share, (owner + 1) * share)
            near = me_blk ^ owner
            piece = jnp.where(far % 2 == 0, own_ref[far // 2, near], other_ref[far // 2, near])
            corner_ref[tile, rows, :] = piece
            if tile * lanes < n:
                work_ref[rows, tile * lanes : (tile + 1) * lanes] = piece
    inv_ref[...] = jnp.zeros_like(inv_ref)
    for low in range(0, n, PANEL):
        high = low + PANEL
        inverse = inverse_factor(work_ref[low:high, low:high])
        inv_ref[low:high, low:high] = inverse
        if low:
            inv_ref[low:high, :low] = dot(inverse, inv_ref[low:high, :low], ((1,), (0,)))
        if high < n:
            upper = dot(inverse, work_ref[low:high, high:], ((1,), (0,)))
            work_ref[high:, high:] -= dot(upper, upper, ((0,), (0,)))
            inv_ref[high:, :high] -= dot(upper, inv_ref[low:high, :high], ((0,), (0,)))


def inverse_of_factor(place, own, other):
    quads, owners, share, lanes = own.shape
    n = owners * share
    return pl.pallas_call(
        factor_kernel,
        out_shape=(
            jax.ShapeDtypeStruct((n, n), jnp.float32),
            jax.ShapeDtypeStruct((2 * quads, n, lanes), jnp.float32),
        ),
        in_specs=[pl.BlockSpec(memory_space=pltpu.SMEM)]
        + [pl.BlockSpec(memory_space=pltpu.VMEM)] * 2,
        out_specs=(pl.BlockSpec(memory_space=pltpu.VMEM), pl.BlockSpec(memory_space=pltpu.VMEM)),
        scratch_shapes=[pltpu.VMEM((n, n), jnp.float32)],
        compiler_params=pltpu.CompilerParams(vmem_limit_bytes=32 * 2**20),
        cost_estimate=pl.CostEstimate(
            flops=10**9, bytes_accessed=6 * 2**20, transcendentals=0
        ),
    )(place, own, other)


def swap(x, axis, d):
    return lax.ppermute(x, axis, [(i, i ^ d) for i in range(lax.axis_size(axis))])


def exchange(pieces, core):
    kept = [swap(x, "grp", 2 * d) if d else x for d, x in enumerate(pieces)]
    other = [lax.dynamic_index_in_dim(x, 1 - core, 0, keepdims=False) for x in kept]
    return kept, [swap(x, "grp", 1) for x in other]


def parity(x):
    for shift in (4, 2, 1):
        x = x ^ lax.shift_right_logical(x, shift)
    return x & 1


def split_kernel(quads, per, place_ref, sign_ref, extra_ref, *refs):
    sources, outs = refs[: quads * per], refs[quads * per :]
    rows = sign_ref.shape[0]
    sign = sign_ref[...].astype(jnp.float32)
    for d, out in enumerate(outs):
        half = out.shape[2]
        for s, source in enumerate(sources[d * per : (d + 1) * per]):
            signed = source[...] * sign
            for part in range(2):
                core, at = divmod((2 * s + part) * LANES, half)
                out[core, :rows, at : at + LANES] = signed[:, part * LANES : (part + 1) * LANES]
        if out.shape[1] > rows:
            out[0, rows:, :] = extra_ref[...]
            out[1, rows:, :] = extra_ref[...]


def split_columns(zed, matrix, signs, extra, quads, first, part):
    rows = matrix.shape[0]
    block = 2 * LANES
    per = 2 * part // block
    reads = [
        pl.BlockSpec(
            (rows, block), lambda i, z, d=d, s=s: (0, first // block + (z[0] ^ d) * per + s)
        )
        for d in range(quads)
        for s in range(per)
    ]
    shape = (2, rows + (8 if extra.shape[1] == part else 0), part)
    return pl.pallas_call(
        functools.partial(split_kernel, quads, per),
        grid_spec=pltpu.PrefetchScalarGridSpec(
            num_scalar_prefetch=1,
            grid=(1,),
            in_specs=[pl.BlockSpec((rows, 1), lambda i, z: (0, 0))]
            + [pl.BlockSpec(extra.shape, lambda i, z: (0, 0))]
            + reads,
            out_specs=[pl.BlockSpec(shape, lambda i, z: (0, 0, 0))] * quads,
        ),
        out_shape=[jax.ShapeDtypeStruct(shape, jnp.float32)] * quads,
        compiler_params=pltpu.CompilerParams(vmem_limit_bytes=32 * 2**20),
        cost_estimate=pl.CostEstimate(
            flops=2 * quads * rows * part,
            bytes_accessed=16 * quads * rows * part,
            transcendentals=0,
        ),
    )(zed.reshape(1), signs.reshape(rows, 1), extra, *[matrix] * (quads * per))


def sample_first_kernel(scale, quads, place_ref, *refs):
    kept, given = refs[:quads], refs[quads : 2 * quads]
    sampled_ref, select_ref, mixed_ref = refs[2 * quads :]
    groups, picked, rows = select_ref.shape
    me = place_ref[0]
    column = lax.broadcasted_iota(jnp.int32, (picked, rows), 1)
    for d in range(quads):
        for e in range(2):
            lists = given[d][rows:, :] if e else kept[d][0, rows:, :]
            wanted = lists.T[:, :1].astype(jnp.int32)
            group = me ^ (2 * d + e)
            odd = parity(jnp.maximum(wanted, 0) & column) ^ parity(group & me)
            select = jnp.where(wanted >= 0, 1 - 2 * odd, 0)
            select_ref[group] = select.astype(jnp.float32).astype(jnp.bfloat16)
    sample_kernel(scale, quads, False, place_ref, select_ref, *kept, *given, sampled_ref, mixed_ref)


def sample_first(me, rows, picked, kept, given):
    quads = len(kept)
    groups = 2 * quads
    sent, block = given[0].shape

    def whole(*shape):
        return pl.BlockSpec(shape, lambda s, p: (0,) * len(shape))

    shapes = [(groups, picked, block), (groups, picked, rows)]
    return pl.pallas_call(
        functools.partial(sample_first_kernel, 1.0 / math.sqrt(groups * rows), quads),
        grid_spec=pltpu.PrefetchScalarGridSpec(
            num_scalar_prefetch=1,
            grid=(1,),
            in_specs=[pl.BlockSpec((1, sent, block), lambda s, p: (p[0] % 2, 0, 0))] * quads
            + [whole(sent, block)] * quads,
            out_specs=[whole(*shape) for shape in shapes],
            scratch_shapes=[pltpu.VMEM((groups, rows, block), jnp.float32)],
        ),
        out_shape=[
            jax.ShapeDtypeStruct(shapes[0], jnp.float32),
            jax.ShapeDtypeStruct(shapes[1], jnp.bfloat16),
        ],
        compiler_params=pltpu.CompilerParams(vmem_limit_bytes=24 * 2**20),
        cost_estimate=pl.CostEstimate(
            flops=6 * groups * picked * rows * block, bytes_accessed=4 * 2**20, transcendentals=0
        ),
    )(me.reshape(1), *kept, *given)


def sample_kernel(scale, quads, has_early, place_ref, select_ref, *refs):
    mixed_ref = refs[-1]
    groups, rows, width = mixed_ref.shape
    kept, given = refs[:quads], refs[quads : 2 * quads]
    early_ref = refs[2 * quads] if has_early else None
    sampled_ref = refs[2 * quads + has_early]
    backs = refs[2 * quads + has_early + 1 : -1]
    step = 16 if width <= 128 else 8

    def mix(r, carry):
        at = pl.ds(pl.multiple_of(r * step, step), step)
        parts = []
        for d in range(quads):
            parts += [kept[d][0, at, :], given[d][at, :]]
        level = 1
        while level < groups:
            new = list(parts)
            for k in range(groups):
                if not k & level:
                    new[k] = parts[k] + parts[k | level]
                    new[k | level] = parts[k] - parts[k | level]
            parts = new
            level *= 2
        for k in range(groups):
            mixed_ref[k, at, :] = parts[k]
        return carry

    lax.fori_loop(0, rows // step, mix, 0)
    zed = place_ref[0] // 2
    for d in range(quads):
        for c in range(2):
            group = 2 * (zed ^ d) + c
            left = select_ref[group]
            value = mixed_ref[group]
            total = None
            for _ in range(3):
                high = value.astype(jnp.bfloat16)
                term = jnp.dot(left, high, preferred_element_type=jnp.float32)
                total = term if total is None else total + term
                value = value - high.astype(jnp.float32)
            total = total * scale
            if early_ref is None:
                sampled_ref[group] = total
                continue
            early = early_ref[group]
            done = early.shape[1]
            sampled_ref[group, :, :done] = early
            sampled_ref[group, :, done:] = total
            backs[d][c, :, :done] = early
            backs[d][c, :, done:] = total


def sample(me, select, kept, given, early):
    groups, picked, rows = select.shape
    quads = groups // 2
    block = given[0].shape[1]

    def whole(*shape):
        return pl.BlockSpec(shape, lambda s, p: (0,) * len(shape))

    in_specs = [whole(groups, picked, rows)]
    in_specs += [pl.BlockSpec((1, rows, block), lambda s, p: (p[0] % 2, 0, 0))] * quads
    in_specs += [whole(rows, block)] * quads
    in_specs.append(whole(*early.shape))
    part = block + early.shape[2]
    shapes = [(groups, picked, part)] + [(2, picked, part)] * quads
    return pl.pallas_call(
        functools.partial(sample_kernel, 1.0 / math.sqrt(groups * rows), quads, True),
        grid_spec=pltpu.PrefetchScalarGridSpec(
            num_scalar_prefetch=1,
            grid=(1,),
            in_specs=in_specs,
            out_specs=[whole(*shape) for shape in shapes],
            scratch_shapes=[pltpu.VMEM((groups, rows, block), jnp.float32)],
        ),
        out_shape=[jax.ShapeDtypeStruct(shape, jnp.float32) for shape in shapes],
        compiler_params=pltpu.CompilerParams(vmem_limit_bytes=40 * 2**20),
        cost_estimate=pl.CostEstimate(
            flops=6 * groups * picked * rows * block, bytes_accessed=9 * 2**20, transcendentals=0
        ),
    )(me.reshape(1), select, *kept, *given, early)


def gram_kernel(place_ref, rest_ref, *refs):
    leads, out_ref, all_ref = refs[:-2], refs[-2], refs[-1]
    for k, lead in enumerate(leads):
        tile = place_ref[0] ^ k

        @pl.when(tile < NPAN)
        def _():
            at = pl.ds(pl.multiple_of(tile * LANES, LANES), LANES)
            all_ref[:, at] = lead[...]

    out_ref[...] = dot(all_ref[...], rest_ref[...], ((0,), (0,)))


def gram_part(me, rest, leads):
    rows, part = rest.shape
    return pl.pallas_call(
        gram_kernel,
        out_shape=jax.ShapeDtypeStruct((WIDE, part), jnp.float32),
        in_specs=[pl.BlockSpec(memory_space=pltpu.SMEM)]
        + [pl.BlockSpec(memory_space=pltpu.VMEM)] * (1 + len(leads)),
        out_specs=pl.BlockSpec(memory_space=pltpu.VMEM),
        scratch_shapes=[pltpu.VMEM((rows, WIDE), jnp.float32)],
        compiler_params=pltpu.CompilerParams(vmem_limit_bytes=36 * 2**20),
        cost_estimate=pl.CostEstimate(
            flops=12 * rows * WIDE * part, bytes_accessed=8 * 2**20, transcendentals=0
        ),
    )(me.reshape(1), rest, *leads)


def pack_kernel(place_ref, tile_ref, *refs):
    out_ref, given_ref = refs[-1], refs[-2]
    kept = refs[:-2]
    quads = len(kept)
    places, per, width = out_ref.shape
    groups = 2 * quads
    rest = width // groups - LANES
    me = place_ref[0]

    def fill(q, carry):
        tile = tile_ref[q]
        at = pl.ds(pl.multiple_of(jnp.maximum(tile, 0) * per, per), per)
        for d in range(quads):
            for e in range(2):
                rows = given_ref[d, at, :] if e else kept[d][0, at, :]
                rows = jnp.where(tile >= 0, rows, 0.0)
                far = me ^ (2 * d + e)
                where = pl.ds(pl.multiple_of(far * LANES, LANES), LANES)
                out_ref[q, :, where] = rows[:, :LANES]
                column = groups * LANES + far * rest
                where = pl.ds(pl.multiple_of(column, LANES), rest)
                out_ref[q, :, where] = rows[:, LANES:]
        return carry

    lax.fori_loop(0, places, fill, 0)


def pack(me, tile_of, kept, given, per):
    places = tile_of.shape[0]
    quads, picked, part = given.shape
    width = 2 * quads * part
    whole = (quads, picked, part)
    return pl.pallas_call(
        pack_kernel,
        grid_spec=pltpu.PrefetchScalarGridSpec(
            num_scalar_prefetch=2,
            grid=(1,),
            in_specs=[pl.BlockSpec((1, picked, part), lambda s, p, t: (p[0] % 2, 0, 0))] * quads
            + [pl.BlockSpec(whole, lambda s, p, t: (0, 0, 0))],
            out_specs=pl.BlockSpec((places, per, width), lambda s, p, t: (0, 0, 0)),
        ),
        out_shape=jax.ShapeDtypeStruct((places, per, width), jnp.float32),
        compiler_params=pltpu.CompilerParams(vmem_limit_bytes=32 * 2**20),
        cost_estimate=pl.CostEstimate(flops=0, bytes_accessed=8 * 2**20, transcendentals=0),
    )(me.reshape(1), tile_of, *kept, given)


def halves(x):
    high = x.astype(jnp.bfloat16)
    return high, (x - high.astype(jnp.float32)).astype(jnp.bfloat16)


def product(weights, gram):
    high, low = halves(gram)

    def term(a, b):
        return jnp.dot(a, b, preferred_element_type=jnp.float32)

    return term(weights[0], high) + (term(weights[0], low) + term(weights[1], high))


def by_turn(value, owners):
    rows, columns = value.shape
    value = value.reshape(owners, rows // owners, columns)
    return jnp.swapaxes(value, 0, 1).reshape(rows, columns)


def lead_kernel(
    scale, owners, place_ref, current_ref, weights_ref, inverse_ref, gram_ref, trailing_ref, top_ref
):
    step = pl.program_id(0)
    gram = jnp.concatenate([gram_ref[0], gram_ref[1]], axis=1)
    taken = product(halves(weights_ref[...]), gram)
    trailing_ref[...] = by_turn(current_ref[...] - taken, owners)

    @pl.when(step == 0)
    def _():
        top_ref[...] = jnp.zeros_like(top_ref)

    @pl.when(step == place_ref[0])
    def _():
        top = dot(inverse_ref[...], gram, ((1,), (0,)))
        row = lax.broadcasted_iota(jnp.int32, top.shape, 0)
        column = lax.broadcasted_iota(jnp.int32, top.shape, 1) + step * top.shape[1]
        top_ref[...] = jnp.where(column >= row // PANEL * PANEL, top, 0.0) * scale


def rest_kernel(
    scale, owners, before, place_ref, weights_ref, lead_ref, current_any, inverse_any, gram_any, _,
    trailing_ref, top_ref, split_ref, current_ref, inverse_ref, gram_ref, out_ref, sems, sent
):
    step = pl.program_id(0)
    steps, n, part = gram_ref.shape
    slot = lax.rem(step, 2)

    def columns(step):
        return pl.ds(pl.multiple_of(before + step * part, LANES), part)

    def fetch(step):
        return (
            pltpu.make_async_copy(gram_any.at[step], gram_ref.at[step], sems.at[0, step]),
            pltpu.make_async_copy(
                current_any.at[:, columns(step)], current_ref.at[step], sems.at[1, step]
            ),
        )

    inverse = pltpu.make_async_copy(inverse_any, inverse_ref, sems.at[0, steps])

    def send(step, slot):
        return pltpu.make_async_copy(
            out_ref.at[slot], trailing_ref.at[:, columns(step)], sent.at[slot]
        )

    @pl.when(step == 0)
    def _():
        for k in range(steps):
            for copy in fetch(k):
                copy.start()
        inverse.start()
        split_ref[0], split_ref[1] = halves(weights_ref[...])
        top_ref[...] = lead_ref[...]

    for copy in fetch(step):
        copy.wait()

    @pl.when(step >= 2)
    def _():
        send(step - 2, slot).wait()

    taken = product((split_ref[0], split_ref[1]), gram_ref[step])
    out_ref[slot] = by_turn(current_ref[step] - taken, owners)
    send(step, slot).start()

    @pl.when(step == steps - 1)
    def _():
        inverse.wait()
        wide = top_ref.shape[1]
        tile = (place_ref[0] * wide - before) // LANES

        @pl.when(tile >= 0)
        def _():
            gram = []
            for s in range(wide // LANES):
                block, at = (tile + s) // (part // LANES), lax.rem(tile + s, part // LANES)
                gram.append(gram_ref[block, :, pl.ds(pl.multiple_of(at * LANES, LANES), LANES)])
            gram = jnp.concatenate(gram, axis=1)
            half = n // 2
            top_ref[:half] = scale * dot(inverse_ref[:half, :half], gram[:half], ((1,), (0,)))
            top_ref[half:] = scale * dot(inverse_ref[half:], gram, ((1,), (0,)))

        send(step - 1, 1 - slot).wait()
        send(step, slot).wait()


def eliminate(scale, me_blk, owners, current, weights, inverse, corner, rest):
    rows, width = current.shape
    wide = width // owners
    groups, n, lanes = corner.shape
    part = rest.shape[2]
    before = groups * lanes

    def whole(*shape):
        return pl.BlockSpec(shape, lambda s, p: (0,) * len(shape))

    out_shape = [
        jax.ShapeDtypeStruct((rows, width), jnp.float32),
        jax.ShapeDtypeStruct((n, wide), jnp.float32),
    ]
    held = pl.BlockSpec(memory_space=pltpu.VMEM)
    columns = pl.BlockSpec((rows, wide), lambda s, p: (0, s))
    trailing, top = pl.pallas_call(
        functools.partial(lead_kernel, scale, owners),
        grid_spec=pltpu.PrefetchScalarGridSpec(
            num_scalar_prefetch=1,
            grid=(before // wide,),
            in_specs=[
                columns,
                held,
                held,
                pl.BlockSpec((wide // lanes, n, lanes), lambda s, p: (s, 0, 0)),
            ],
            out_specs=[columns, whole(n, wide)],
        ),
        out_shape=out_shape,
        compiler_params=pltpu.CompilerParams(vmem_limit_bytes=20 * 2**20),
        cost_estimate=pl.CostEstimate(
            flops=6 * rows * n * before, bytes_accessed=8 * 2**20, transcendentals=0
        ),
    )(me_blk.reshape(1), current, weights, inverse, corner)
    some = pl.BlockSpec(memory_space=pl.ANY)
    return pl.pallas_call(
        functools.partial(rest_kernel, scale, owners, before),
        grid_spec=pltpu.PrefetchScalarGridSpec(
            num_scalar_prefetch=1,
            grid=(groups,),
            in_specs=[held, held] + [some] * 4,
            out_specs=[some, whole(n, wide)],
            scratch_shapes=[
                pltpu.VMEM((2, rows, n), jnp.bfloat16),
                pltpu.VMEM((groups, rows, part), jnp.float32),
                pltpu.VMEM((n, n), jnp.float32),
                pltpu.VMEM((groups, n, part), jnp.float32),
                pltpu.VMEM((2, rows, part), jnp.float32),
                pltpu.SemaphoreType.DMA((2, groups + 1)),
                pltpu.SemaphoreType.DMA((2,)),
            ],
        ),
        out_shape=out_shape,
        input_output_aliases={6: 0},
        compiler_params=pltpu.CompilerParams(vmem_limit_bytes=44 * 2**20),
        cost_estimate=pl.CostEstimate(
            flops=6 * rows * n * (width - before), bytes_accessed=16 * 2**20, transcendentals=0
        ),
    )(me_blk.reshape(1), weights, top, current, inverse, rest, trailing)


def body(matrix, signs, tile_rows, tile_owner):
    rows_dev, width = matrix.shape
    groups = lax.axis_size("grp")
    owners = lax.axis_size("blk")
    me = lax.axis_index("grp")
    me_blk = lax.axis_index("blk")
    zed, core = me // 2, me % 2
    quads = groups // 2
    tiles = tile_owner.shape[1]
    per_source = TILE // owners
    picked = tiles * per_source
    part = width // groups

    wanted = tile_rows[0].reshape(tiles, per_source, owners)
    selector = jnp.arange(owners, dtype=jnp.int32) == me_blk
    wanted = jnp.sum(jnp.where(selector, wanted, 0), axis=2).reshape(1, picked)
    wanted = jnp.broadcast_to(wanted.astype(jnp.float32), (8, picked))
    pieces = split_columns(zed, matrix, signs, wanted, quads, 0, LANES)
    first = exchange(pieces, core)
    pieces = split_columns(zed, matrix, signs, wanted, quads, groups * LANES, part - LANES)
    later = exchange(pieces, core)
    lead, select = sample_first(me, rows_dev, picked, *first)

    flat = lead.reshape(groups * picked, LANES)
    leads = []
    for d in range(quads):
        mine = swap(flat, "grp", 2 * d) if d else flat
        leads += [mine, swap(mine, "grp", 1)]
    sampled, *backs = sample(me, select, *later, lead)
    partial = gram_part(me, sampled.reshape(groups * picked, part), leads)

    share = WIDE // owners
    partial = partial.reshape(owners, share, part)
    partial, *backs = lax.optimization_barrier((partial, *backs))
    summands = lax.all_to_all(partial, "blk", 0, 0, tiled=True)
    backs = [swap(backs[d], "grp", 2 * d) if d else backs[d] for d in range(quads)]
    give = jnp.stack([lax.dynamic_index_in_dim(x, 1 - core, 0, keepdims=False) for x in backs])
    give = swap(give, "grp", 1)
    owner_list = tile_owner[0]
    same = owner_list[:, None] == owner_list[None, :]
    order = jnp.arange(tiles, dtype=jnp.int32)
    rank = jnp.sum((same & (order[None, :] < order[:, None])).astype(jnp.int32), axis=1)
    place = owner_list * MAXT + rank
    hit = place[None, :] == jnp.arange(owners * MAXT, dtype=jnp.int32)[:, None]
    tile_of = jnp.max(jnp.where(hit, order[None, :], -1), axis=1)
    outgoing = pack(me, tile_of, backs, give, per_source)
    outgoing = outgoing.reshape(owners, MAXT * per_source, width)
    outgoing, summands = lax.optimization_barrier((outgoing, summands))
    gram = jnp.sum(summands, axis=0)
    rest = lax.all_gather(gram[:, LANES:], ("grp", "blk"), tiled=True)
    rest = rest.reshape(groups, WIDE, part - LANES)
    corner = gram[:, :LANES][None]
    for axis, strides in (("blk", (1, 2, 3)), ("blk", (4, 8, 12)), ("grp", (2, 4, 6))):
        corner = jnp.stack([corner] + [swap(corner, axis, d) for d in strides])
        corner = corner.reshape(-1, share, LANES)
        if strides == (4, 8, 12):
            corner, outgoing = lax.optimization_barrier((corner, outgoing))
    corner = corner.reshape(quads, owners, share, LANES)
    inverse, corner = inverse_of_factor(jnp.stack([me, me_blk]), corner, swap(corner, "grp", 1))

    current = lax.all_to_all(outgoing, "blk", 0, 0, tiled=True)
    current = current.reshape(MAXT * TILE, width)

    basis = dot(current[:, :WIDE], inverse, ((1,), (1,)))
    weights = dot(basis, inverse, ((1,), (0,)))
    scale = 1.0 / math.sqrt(groups * owners * TILE)
    trailing, top = eliminate(scale, me_blk, owners, current, weights, inverse, corner, rest)
    return (top, trailing)


def solution(mesh):
    in_specs = (P(("grp", "blk"), None), P(("grp", "blk")), P("grp", None, None), P("grp", None))
    out_specs = (P(None, "blk"), P(("grp", "blk"), None))
    return jax.shard_map(body, mesh=mesh, in_specs=in_specs, out_specs=out_specs, check_vma=False)
```
